32 devices in a mesh: ctx: 8 (over y, x, core), head: 4 (over z).
Axes of the slice: x: 2, y: 2, z: 4, core: 2. Of those that a mesh axis runs over, the one named last changes fastest.
Arguments:
- q_nope: bfloat16 [2048, 2048], P('ctx', 'head'), may hold values from -5 to 5
- q_rope: bfloat16 [2048, 1024], P('ctx', 'head'), may hold values from -320 to 320
- latent: bfloat16 [2048, 512], P('ctx'), may hold values from -5 to 5
- rope_keys: bfloat16 [2048, 64], P('ctx'), may hold values from -4.5 to 4.5
- out_grad: bfloat16 [2048, 2048], P('ctx', 'head'), may hold values from -96 to 96
- up_keys: bfloat16 [512, 2048], P(None, 'head'), may hold values from -0.25 to 0.25
- up_values: bfloat16 [512, 2048], P(None, 'head'), may hold values from -0.25 to 0.25
- group_order: int32 [16], replicated, may hold values from 0 to 15, each once
Outputs:
- grad_q_nope: bfloat16 [2048, 2048], P('ctx', 'head')
- grad_q_rope: bfloat16 [2048, 1024], P('ctx', 'head')
- grad_latent: float32 [2048, 512], P('ctx')
- grad_rope: float32 [2048, 64], P('ctx')
- grad_up_keys: float32 [512, 2048], P('ctx', 'head')
- grad_up_values: float32 [512, 2048], P('ctx', 'head')
The draws below stay inside these ranges and needn't reach their ends.
Inputs may be any that keep to these rules, and one draw needn't show every extreme that they name: `group_order`: each group place appears once.
All inputs are finite; a program needn't handle non-finite values.
Results may differ from the reference program's by a relative error of at most 0.0087.
Values may be sent and summed in bfloat16 or wider, within the bound.
No kernel may reach another device: no remote copies, remote signals or barrier semaphores. Data moves between devices by JAX's collectives and lax.ppermute only.
A program may use at most 128 MiB of HBM per device.

```python
import jax
import jax.numpy as jnp
from jax import lax

LATENT = 512
ROPE = 64
HEAD_DIM = 128
HEADS = 16
SEQ = 2048
GROUP = 128
GROUPS = 16


def rope_base(key):
    return jnp.clip(jax.random.normal(jax.random.fold_in(key, 11), (SEQ, ROPE), jnp.float32), -4.0, 4.0)


def draw_rope_keys(key, part):
    base = rope_base(key)
    return base.astype(jnp.bfloat16)


def draw_q_rope(key, part):
    values = jnp.clip(jax.random.normal(jax.random.fold_in(key, 23), (SEQ, HEADS * ROPE), jnp.float32), -4.0, 4.0)
    return values.astype(jnp.bfloat16)


def steps_of(stream_key, extent, shards, smallest, top_value):
    gain = 1.0
    for axis_at, parts in shards:
        steps = jax.random.uniform(jax.random.fold_in(jax.random.fold_in(stream_key, 6), axis_at), (parts,), jnp.float32, smallest / len(shards), top_value / len(shards))
        gain = gain * jnp.repeat(jnp.exp(steps), extent[axis_at] // parts).reshape((-1,) + (1,) * (len(extent) - 1 - axis_at))
    return gain


def noise(key, dims, width, limit, split=(), held_as=jnp.bfloat16):
    level = steps_of(key, dims, split, -0.22, 0.18) if split else 1.0
    result = jax.random.normal(key, dims, jnp.float32) * width * level
    return jnp.minimum(jnp.maximum(result, -limit), limit).astype(held_as)


def setup_inputs(seed: int = 0) -> dict:
    splits = jax.random.split(jax.random.key(seed), 9)
    q_nope = noise(splits[0], (SEQ, HEADS * HEAD_DIM), 1.0, 5.0, ((0, 8), (1, 4)))
    q_rope = draw_q_rope(jax.random.fold_in(splits[8], 71), 0)
    latent = noise(splits[2], (SEQ, LATENT), 1.0, 5.0, ((0, 8),))
    rope_keys = draw_rope_keys(jax.random.fold_in(splits[8], 71), 0)
    out_grad = noise(splits[4], (SEQ, HEADS * HEAD_DIM), 16.0, 96.0, ((0, 8), (1, 4)))
    up_keys = noise(splits[5], (LATENT, HEADS * HEAD_DIM), LATENT ** -0.5, 0.25, ((1, 4),))
    up_values = noise(splits[6], (LATENT, HEADS * HEAD_DIM), LATENT ** -0.5, 0.25, ((1, 4),))
    group_order = jax.random.permutation(splits[7], GROUPS).astype(jnp.int32)
    return {"q_nope": q_nope, "q_rope": q_rope, "latent": latent, "rope_keys": rope_keys, "out_grad": out_grad, "up_keys": up_keys, "up_values": up_values, "group_order": group_order}


NEG_LARGE = -1e30


def reference(q_nope, q_rope, latent, rope_keys, out_grad, up_keys, up_values, group_order):
    seq_len = q_nope.shape[0]
    rows = jnp.arange(seq_len, dtype=jnp.int32)
    place = group_order[rows // GROUP] * GROUP + rows % GROUP
    visible = place[None, :] <= place[:, None]
    scale = (HEAD_DIM + ROPE) ** -0.5
    keys_all = jnp.dot(latent, up_keys, preferred_element_type=jnp.float32).astype(jnp.bfloat16)
    values_all = jnp.dot(latent, up_values, preferred_element_type=jnp.float32).astype(jnp.bfloat16)
    head_count = q_nope.shape[1] // HEAD_DIM

    def one_head(index):
        query_nope = lax.dynamic_slice_in_dim(q_nope, index * HEAD_DIM, HEAD_DIM, 1)
        query_rope = lax.dynamic_slice_in_dim(q_rope, index * ROPE, ROPE, 1)
        grad_head = lax.dynamic_slice_in_dim(out_grad, index * HEAD_DIM, HEAD_DIM, 1)
        key_rows = lax.dynamic_slice_in_dim(keys_all, index * HEAD_DIM, HEAD_DIM, 1)
        value_rows = lax.dynamic_slice_in_dim(values_all, index * HEAD_DIM, HEAD_DIM, 1)
        score = jnp.dot(query_nope, key_rows.T, preferred_element_type=jnp.float32)
        score = (score + jnp.dot(query_rope, rope_keys.T, preferred_element_type=jnp.float32)) * scale
        masked = jnp.where(visible, score, NEG_LARGE)
        row_top = jnp.max(masked, axis=1, keepdims=True)
        expd = jnp.where(visible, jnp.exp(masked - row_top), 0.0)
        attn = expd / jnp.sum(expd, axis=1, keepdims=True)
        dattn = jnp.dot(grad_head, value_rows.T, preferred_element_type=jnp.float32)
        delta = jnp.sum(attn * dattn, axis=1, keepdims=True)
        dscore = (attn * (dattn - delta)).astype(jnp.bfloat16)
        grad_nope = (jnp.dot(dscore, key_rows, preferred_element_type=jnp.float32) * scale).astype(jnp.bfloat16)
        grad_qrope = (jnp.dot(dscore, rope_keys, preferred_element_type=jnp.float32) * scale).astype(jnp.bfloat16)
        dkeys = (jnp.dot(dscore.T, query_nope, preferred_element_type=jnp.float32) * scale).astype(jnp.bfloat16)
        dvalues = jnp.dot(attn.astype(jnp.bfloat16).T, grad_head, preferred_element_type=jnp.float32).astype(jnp.bfloat16)
        drope = jnp.dot(dscore.T, query_rope, preferred_element_type=jnp.float32) * scale
        return grad_nope, grad_qrope, dkeys, dvalues, drope

    stacked = lax.map(one_head, jnp.arange(head_count, dtype=jnp.int32))

    def flatten(block):
        return jnp.transpose(block, (1, 0, 2)).reshape(seq_len, -1)

    grad_q_nope = flatten(stacked[0])
    grad_q_rope = flatten(stacked[1])
    dkeys_all = flatten(stacked[2])
    dvalues_all = flatten(stacked[3])
    grad_rope = jnp.sum(stacked[4], axis=0)
    grad_latent = jnp.dot(dkeys_all, up_keys.T, preferred_element_type=jnp.float32)
    grad_latent = grad_latent + jnp.dot(dvalues_all, up_values.T, preferred_element_type=jnp.float32)
    grad_up_keys = jnp.dot(latent.T, dkeys_all, preferred_element_type=jnp.float32)
    grad_up_values = jnp.dot(latent.T, dvalues_all, preferred_element_type=jnp.float32)
    return grad_q_nope, grad_q_rope, grad_latent, grad_rope, grad_up_keys, grad_up_values
```

```python
import functools
import math

import jax
import jax.numpy as jnp
from jax import lax
from jax.experimental import pallas as pl
from jax.experimental.pallas import tpu as pltpu
from jax.sharding import PartitionSpec as P

ROPE = 64
HEAD_DIM = 128
H_DEV = 4
GROUP = 128
LANES = 128
TILE = 2 * GROUP
CHUNK = 512
SCALE = (HEAD_DIM + ROPE) ** (-0.5)
SCALE2 = SCALE * math.log2(math.e)
NEG_LARGE = -1e30

F32 = jnp.float32
BF16 = jnp.bfloat16
NT = (((1,), (1,)), ((), ()))
TN = (((0,), (0,)), ((), ()))
NN = (((1,), (0,)), ((), ()))
VMEM = pl.BlockSpec(memory_space=pltpu.VMEM)
SMEM = pl.BlockSpec(memory_space=pltpu.SMEM)


def dot(a, b, dims=NN):
    return lax.dot_general(a, b, dims, preferred_element_type=F32)


def call(body, outs, ins, scratch=(), mib=16, flops=0):
    moved = sum(math.prod(x.shape) * x.dtype.itemsize for x in (*outs, *ins))
    return pl.pallas_call(
        body,
        out_shape=list(outs),
        in_specs=[SMEM if x.dtype == jnp.int32 else VMEM for x in ins],
        out_specs=[VMEM] * len(outs),
        scratch_shapes=list(scratch),
        compiler_params=pltpu.CompilerParams(vmem_limit_bytes=mib << 20),
        cost_estimate=pl.CostEstimate(flops=flops, bytes_accessed=moved, transcendentals=0),
    )(*ins)


def shape(*dims, dtype=BF16):
    return jax.ShapeDtypeStruct(dims, dtype)


def lanes_of(index, width=LANES):
    return pl.ds(pl.multiple_of(index * width, LANES), width)


def rows_of(index, count):
    return pl.ds(pl.multiple_of(index * count, count), count)


def halves(block):
    half = block.shape[0] // 2
    return jnp.concatenate([block[:half], block[half:]], axis=1)


def pack_body(r, width, me, q_nope, q_rope, grad, latent, rope, up_keys, up_values, *pieces):
    head_here = me[0] // r
    half = width // 2
    for k in range(H_DEV):
        out = pieces[k]
        head = head_here ^ k
        out[0:width] = q_nope[:, lanes_of(head)]
        out[width : 2 * width] = grad[:, lanes_of(head)]
        both = q_rope[:, lanes_of(head // 2)]
        mine = jnp.where(head % 2 == 0, both[:, :ROPE], both[:, ROPE:])
        out[2 * width : 2 * width + half] = halves(mine)
        at = 2 * width + half
        out[at : at + width] = dot(latent[...], up_keys[:, lanes_of(head)]).astype(BF16)
        out[at + width : at + 2 * width] = dot(latent[...], up_values[:, lanes_of(head)]).astype(
            BF16
        )
        out[at + 2 * width : at + 2 * width + half] = halves(rope[...])


def attend_body(n, r, width, me_ref, order, *refs):
    pieces, refs = refs[:n], refs[n:]
    keep, send, *dq_out = refs[: 2 + H_DEV]
    (kcat, kcat_t, vals, qcat, grads, scores, dattn, tops, acc, acc_rope, dq_t, dq_all, table) = refs[
        2 + H_DEV :
    ]
    me = me_ref[0]
    parity = me % 2
    groups = width // GROUP
    half = width // 2
    kv_at = 2 * width + half
    local = H_DEV * groups

    for m in range(n):
        piece = pieces[m]
        for g in range(groups):
            place = order[(me ^ m) * groups + g]
            key = piece[kv_at + g * GROUP : kv_at + (g + 1) * GROUP, :]
            packed = piece[kv_at + 2 * width : kv_at + 2 * width + half, :]
            rope = packed[:, g * ROPE : (g + 1) * ROPE]
            wide = jnp.concatenate([rope, jnp.zeros_like(rope)], axis=1)
            at = rows_of(place, GROUP)
            kcat[at, 0:LANES] = key
            kcat[at, LANES : 2 * LANES] = wide
            kcat_t[0:LANES, lanes_of(place)] = key.T
            kcat_t[LANES : 2 * LANES, lanes_of(place)] = wide.T
            first = kv_at + width + g * GROUP
            vals[at, :] = piece[first : first + GROUP, :]

    places = [order[(me ^ (k * r)) * groups + g] for k in range(H_DEV) for g in range(groups)]
    ranks = [sum((other < mine).astype(jnp.int32) for other in places) for mine in places]
    for k in range(H_DEV):
        piece = pieces[k * r]
        for g in range(groups):
            rank = ranks[k * groups + g]
            table[rank] = places[k * groups + g]
            at = rows_of(rank, GROUP)
            qcat[at, 0:LANES] = piece[g * GROUP : (g + 1) * GROUP, :]
            rope = piece[2 * width : 2 * width + half, g * ROPE : (g + 1) * ROPE]
            qcat[at, LANES : 2 * LANES] = jnp.concatenate([rope, jnp.zeros_like(rope)], axis=1)
            grads[at, :] = piece[width + g * GROUP : width + (g + 1) * GROUP, :]

    acc[...] = jnp.zeros_like(acc)
    acc_rope[...] = jnp.zeros_like(acc_rope)

    def tile(t, carry):
        q_rows = rows_of(t, TILE)
        query = qcat[q_rows, :]
        grad = grads[q_rows, :]
        first, second = table[2 * t], table[2 * t + 1]
        lane = lax.broadcasted_iota(jnp.int32, (1, TILE), 1)
        q_pos = jnp.where(lane < GROUP, first * GROUP + lane, second * GROUP + lane - GROUP)
        chunks = second // (CHUNK // GROUP) + 1

        def scan(c, carry):
            top, total, weighted = carry
            at = rows_of(c, CHUNK)
            raw = dot(kcat[at, :], query, NT)
            k_pos = c * CHUNK + lax.broadcasted_iota(jnp.int32, (CHUNK, TILE), 0)
            raw = jnp.where(k_pos <= q_pos, raw, NEG_LARGE)
            new_top = jnp.maximum(top, jnp.max(raw, axis=0, keepdims=True))
            expd = jnp.exp2((raw - new_top) * SCALE2)
            dat = dot(vals[at, :], grad, NT)
            factor = jnp.exp2((top - new_top) * SCALE2)
            scores[at, :] = expd
            dattn[at, :] = dat
            tops[pl.ds(c, 1), :] = new_top
            total = total * factor + jnp.sum(expd, axis=0, keepdims=True)
            weighted = weighted * factor + jnp.sum(expd * dat, axis=0, keepdims=True)
            return new_top, total, weighted

        start = (
            jnp.full((1, TILE), NEG_LARGE, F32),
            jnp.zeros((1, TILE), F32),
            jnp.zeros((1, TILE), F32),
        )
        top, total, weighted = lax.fori_loop(0, chunks, scan, start)
        inverse = 1.0 / total
        delta = weighted * inverse
        dq_t[...] = jnp.zeros_like(dq_t)

        def grad_step(c, carry):
            at = rows_of(c, CHUNK)
            factor = jnp.exp2((tops[pl.ds(c, 1), :] - top) * SCALE2) * inverse
            attn = scores[at, :] * factor
            dscore = (attn * (dattn[at, :] - delta)).astype(BF16)
            acc[1, at, :] += dot(attn.astype(BF16), grad)
            dk = dot(dscore, query)
            acc[0, at, :] += dk[:, 0:LANES]
            acc_rope[at, :] += dk[:, LANES : 2 * LANES]
            columns = pl.ds(pl.multiple_of(c * CHUNK, CHUNK), CHUNK)
            dq_t[...] += dot(kcat_t[:, columns], dscore)
            return carry

        lax.fori_loop(0, chunks, grad_step, 0)
        dq_all[q_rows, :] = (dq_t[...] * SCALE).T.astype(BF16)
        return carry

    lax.fori_loop(0, local // 2, tile, 0)

    for k in range(H_DEV):
        out = dq_out[k]
        ropes = []
        for g in range(groups):
            at = rows_of(ranks[k * groups + g], GROUP)
            out[g * GROUP : (g + 1) * GROUP, :] = dq_all[at, 0:LANES]
            ropes.append(dq_all[at, LANES : 2 * LANES][:, :ROPE])
        out[width : width + half, :] = jnp.concatenate(ropes, axis=1)

    keep_scale = jnp.where(parity == 0, SCALE, 1.0)
    send_scale = jnp.where(parity == 0, 1.0, SCALE)
    unit = 2 * width + half
    for k in range(H_DEV):
        for pair in range(r // 2):
            base = (k * (r // 2) + pair) * unit
            device = ((me // r) ^ k) * r + 2 * pair
            for p in range(2):
                for g in range(groups):
                    at = rows_of(order[(device + p) * groups + g], GROUP)
                    rows = slice(base + p * width + g * GROUP, base + p * width + (g + 1) * GROUP)
                    keep[rows, :] = acc[parity, at, :] * keep_scale
                    send[rows, :] = (acc[1 - parity, at, :] * send_scale).astype(BF16)
            for out, p in ((keep, parity), (send, 1 - parity)):
                ropes = [
                    acc_rope[rows_of(order[(device + p) * groups + g], GROUP), :][:, :ROPE]
                    for g in range(groups)
                ]
                out[base + 2 * width : base + unit, :] = (
                    jnp.concatenate(ropes, axis=1) * SCALE
                ).astype(out.dtype)


def combine_body(unit, keep, got, *outs):
    for k, out in enumerate(outs):
        rows = slice(k * unit, (k + 1) * unit)
        out[...] = (keep[rows, :] + got[rows, :].astype(F32)).astype(BF16)


def weights_body(n, r, width, rows, me_ref, *refs):
    latents, refs = refs[:n], refs[n:]
    grads, refs = refs[:H_DEV], refs[H_DEV:]
    dqs, refs = refs[:H_DEV], refs[H_DEV:]
    outs, total = refs[:H_DEV], refs[H_DEV]
    me = me_ref[0]
    unit = 2 * width + width // 2
    share = me % r
    value = jnp.zeros(total.shape, F32)
    for m in range(n):
        k, j = m // r, m % r
        there = share ^ j
        first = (there // 2) * unit + (there % 2) * width
        grad = grads[k][pl.ds(pl.multiple_of(first, GROUP), width), :]
        value += dot(latents[m][...], grad, TN)
    total[...] = value
    for k in range(H_DEV):
        device = ((me // r) ^ k) * r + share - share % 2
        size = dqs[k].shape[0]
        outs[k][0:size, :] = dqs[k][...]
        first = pl.multiple_of(device * rows, 2 * rows)
        outs[k][size : size + 2 * rows, :] = total[pl.ds(first, 2 * rows), :].astype(BF16)


def latent_body(r, width, z_size, ids, *refs):
    own, refs = refs[:H_DEV], refs[H_DEV:]
    other, refs = refs[:H_DEV], refs[H_DEV:]
    up_keys, up_values, kept, *refs = refs
    outs, (total, total_rope) = refs[: z_size - 1], refs[z_size - 1 :]
    me, z = ids[0], ids[1]
    parity = me % 2
    mine = pl.ds(pl.multiple_of(parity * width, GROUP), width)
    dkeys, dvalues, key_w, value_w = [], [], [], []
    rope = jnp.zeros((width // 2, LANES), F32)
    value = jnp.zeros(total.shape, F32)
    for k in range(H_DEV):
        head = (me // r) ^ k
        a, b = own[k][mine, :], other[k][mine, :]
        dkey = jnp.where(parity == 0, a, b)
        dvalue = jnp.where(parity == 0, b, a)
        pair = jnp.concatenate([dkey, dvalue], axis=1)
        up = jnp.concatenate([up_keys[:, lanes_of(head)], up_values[:, lanes_of(head)]], axis=1)
        value += dot(pair, up, NT)
        rope += own[k][2 * width : 2 * width + width // 2, :].astype(F32)
    total[...] = value
    total_rope[...] = rope
    tokens = width // z_size
    blocks = total.shape[1] // LANES
    for k in range(z_size):
        out = kept if k == 0 else outs[k - 1]
        part = total[rows_of(z ^ k, tokens), :].astype(out.dtype)
        for i in range(blocks):
            out[i * tokens : (i + 1) * tokens, :] = part[:, i * LANES : (i + 1) * LANES]
        out[blocks * tokens :, :] = total_rope[rows_of(z ^ k, tokens // 2), :].astype(out.dtype)


def sum_body(kept, *refs):
    *got, out = refs
    out[...] = (kept[...] + sum(x[...].astype(F32) for x in got)).astype(BF16)


def finish_body(z_size, width, ids, *refs):
    parts, (grad_latent, grad_rope) = refs[:z_size], refs[z_size:]
    z = ids[1]
    tokens = width // z_size
    blocks = grad_latent.shape[1] // LANES
    for k in range(z_size):
        part = parts[k][...].astype(F32)
        for i in range(blocks):
            grad_latent[rows_of(z ^ k, tokens), i * LANES : (i + 1) * LANES] = part[
                i * tokens : (i + 1) * tokens, :
            ]
        rope = part[blocks * tokens :, :]
        for g in range(2):
            first = pl.multiple_of(g * (width // 2) + (z ^ k) * (tokens // 2), tokens // 2)
            grad_rope[pl.ds(first, tokens // 2), :] = rope[:, g * ROPE : (g + 1) * ROPE]


def unpack_body(r, width, rows, me_ref, *refs):
    own, refs = refs[:H_DEV], refs[H_DEV:]
    other, refs = refs[:H_DEV], refs[H_DEV:]
    grad_q_nope, grad_q_rope, grad_up_keys, grad_up_values = refs
    me = me_ref[0]
    parity = me % 2
    half = width // 2
    at = width + half
    mine = pl.ds(pl.multiple_of(at + parity * rows, rows), rows)
    ropes = []
    for k in range(H_DEV):
        head = (me // r) ^ k
        grad_q_nope[:, lanes_of(head)] = own[k][0:width, :]
        packed = own[k][width:at, :]
        ropes.append(jnp.concatenate([packed[:, :ROPE], packed[:, ROPE:]], axis=0))
        a, b = own[k][mine, :].astype(F32), other[k][mine, :].astype(F32)
        grad_up_keys[:, lanes_of(head)] = jnp.where(parity == 0, a, b)
        grad_up_values[:, lanes_of(head)] = jnp.where(parity == 0, b, a)
    for k in range(0, H_DEV, 2):
        head = (me // r) ^ k
        a, b = ropes[k], ropes[k + 1]
        even = head % 2 == 0
        grad_q_rope[:, lanes_of(head // 2)] = jnp.concatenate(
            [jnp.where(even, a, b), jnp.where(even, b, a)], axis=1
        )


def per_device(q_nope, q_rope, latent, rope_keys, out_grad, up_keys, up_values, group_order):
    width = q_nope.shape[0]
    depth = latent.shape[1]
    n = lax.axis_size("ctx")
    z_size = lax.axis_size("head")
    r = n // H_DEV
    groups = width // GROUP
    half = width // 2
    seq_len = n * width
    me = lax.axis_index("ctx")
    ids = jnp.stack([me, lax.axis_index("head")]).astype(jnp.int32)
    unit = 2 * width + half
    rows = depth // n

    def over_ctx(x, mask):
        return lax.ppermute(x, "ctx", [(i, i ^ mask) for i in range(n)])

    def over_head(x, mask):
        return lax.ppermute(x, "head", [(i, i ^ mask) for i in range(z_size)])

    def across(pieces):
        return [pieces[0]] + [over_ctx(pieces[k], k * r) for k in range(1, H_DEV)]

    def shared(pieces):
        return [over_ctx(p, j) if j else p for p in pieces for j in range(r)]

    pieces = call(
        functools.partial(pack_body, r, width),
        [shape(2 * unit, LANES)] * H_DEV,
        [ids, q_nope, q_rope, out_grad, latent, rope_keys, up_keys, up_values],
        flops=4 * width * depth * H_DEV * HEAD_DIM,
    )
    arrived = across(pieces)
    everyone = shared(arrived)

    later = lax.optimization_barrier((latent, arrived))[0]
    latents = shared([later] + [over_ctx(later, k * r) for k in range(1, H_DEV)])

    queries = H_DEV * width
    outs = call(
        functools.partial(attend_body, n, r, width),
        [
            shape(n // 2 * unit, LANES, dtype=F32),
            shape(n // 2 * unit, LANES),
            *[shape(width + half, LANES)] * H_DEV,
        ],
        [ids, group_order, *everyone],
        scratch=[
            pltpu.VMEM((seq_len, 2 * LANES), BF16),
            pltpu.VMEM((2 * LANES, seq_len), BF16),
            pltpu.VMEM((seq_len, LANES), BF16),
            pltpu.VMEM((queries, 2 * LANES), BF16),
            pltpu.VMEM((queries, LANES), BF16),
            pltpu.VMEM((seq_len, TILE), F32),
            pltpu.VMEM((seq_len, TILE), F32),
            pltpu.VMEM((max(8, seq_len // CHUNK), TILE), F32),
            pltpu.VMEM((2, seq_len, LANES), F32),
            pltpu.VMEM((seq_len, LANES), F32),
            pltpu.VMEM((2 * LANES, TILE), F32),
            pltpu.VMEM((queries, 2 * LANES), BF16),
            pltpu.SMEM((H_DEV * groups,), jnp.int32),
        ],
        mib=40,
        flops=6 * queries * seq_len * (HEAD_DIM + ROPE + HEAD_DIM),
    )
    keep, send, *dqs = outs
    got = over_ctx(send, 1)
    for j in range(2, r, 2):
        summed = keep + got.astype(F32)
        keep, got = summed, over_ctx(summed.astype(BF16), j)
    span = (r // 2) * unit
    whole = call(
        functools.partial(combine_body, span), [shape(span, LANES)] * H_DEV, [keep, got], mib=24
    )
    if r == 2:
        dkv = whole
    else:
        start = (me % r) // 2 * unit
        dkv = [lax.dynamic_slice_in_dim(x, start, unit, 0) for x in whole]
    own = across(dkv)
    other = [over_ctx(x, 1) for x in own]

    late_dqs = lax.optimization_barrier((dqs, own))[0]
    mixed = call(
        functools.partial(weights_body, n, r, width, rows),
        [shape(width + half + 2 * rows, LANES)] * H_DEV,
        [ids, *latents, *whole, *late_dqs],
        scratch=[pltpu.VMEM((depth, LANES), F32)],
        mib=24,
        flops=2 * seq_len * depth * LANES,
    )

    tokens = width // z_size
    z_rows = depth // LANES * tokens + tokens // 2
    kept, *for_planes = call(
        functools.partial(latent_body, r, width, z_size),
        [shape(z_rows, LANES, dtype=F32)] + [shape(z_rows, LANES)] * (z_size - 1),
        [ids, *own, *other, up_keys, up_values],
        scratch=[pltpu.VMEM((width, depth), F32), pltpu.VMEM((half, LANES), F32)],
        flops=4 * width * depth * H_DEV * HEAD_DIM,
    )
    received = [over_head(x, k + 1) for k, x in enumerate(for_planes)]
    (part,) = call(sum_body, [shape(z_rows, LANES)], [kept, *received])
    parts = [part] + [over_head(part, k) for k in range(1, z_size)]
    grad_latent, grad_rope = call(
        functools.partial(finish_body, z_size, width),
        [shape(width, depth, dtype=F32), shape(width, ROPE, dtype=F32)],
        [ids, *parts],
    )

    mixed_own = across(mixed)
    mixed_other = [over_ctx(x, 1) for x in mixed_own]
    grad_q_nope, grad_q_rope, grad_up_keys, grad_up_values = call(
        functools.partial(unpack_body, r, width, rows),
        [
            shape(width, H_DEV * HEAD_DIM),
            shape(width, H_DEV * ROPE),
            shape(rows, H_DEV * HEAD_DIM, dtype=F32),
            shape(rows, H_DEV * HEAD_DIM, dtype=F32),
        ],
        [ids, *mixed_own, *mixed_other],
    )
    return (grad_q_nope, grad_q_rope, grad_latent, grad_rope, grad_up_keys, grad_up_values)


def solution(mesh):
    in_specs = (
        P("ctx", "head"),
        P("ctx", "head"),
        P("ctx", None),
        P("ctx", None),
        P("ctx", "head"),
        P(None, "head"),
        P(None, "head"),
        P(),
    )
    out_specs = (
        P("ctx", "head"),
        P("ctx", "head"),
        P("ctx", None),
        P("ctx", None),
        P("ctx", "head"),
        P("ctx", "head"),
    )
    return jax.shard_map(
        per_device, mesh=mesh, in_specs=in_specs, out_specs=out_specs, check_vma=False
    )
```

```python
import functools
import math

import jax
import jax.numpy as jnp
from jax import lax
from jax.experimental import pallas as pl
from jax.experimental.pallas import tpu as pltpu
from jax.sharding import PartitionSpec as P

ROPE = 64
HEAD_DIM = 128
H_DEV = 4
GROUP = 128
LANES = 128
TILE = 2 * GROUP
CHUNK = 512
SCALE = (HEAD_DIM + ROPE) ** (-0.5)
SCALE2 = SCALE * math.log2(math.e)
NEG_LARGE = -1e30

F32 = jnp.float32
BF16 = jnp.bfloat16
NT = (((1,), (1,)), ((), ()))
TN = (((0,), (0,)), ((), ()))
NN = (((1,), (0,)), ((), ()))
VMEM = pl.BlockSpec(memory_space=pltpu.VMEM)
SMEM = pl.BlockSpec(memory_space=pltpu.SMEM)
HBM = pl.BlockSpec(memory_space=pltpu.HBM)


def dot(a, b, dims=NN):
    return lax.dot_general(a, b, dims, preferred_element_type=F32)


def call(body, outs, ins, scratch=(), mib=16, flops=0, hbm=False):
    held = HBM if hbm else VMEM
    moved = sum(math.prod(x.shape) * x.dtype.itemsize for x in (*outs, *ins))
    return pl.pallas_call(
        body,
        out_shape=list(outs),
        in_specs=[SMEM if x.dtype == jnp.int32 else held for x in ins],
        out_specs=[VMEM] * len(outs),
        scratch_shapes=list(scratch),
        compiler_params=pltpu.CompilerParams(vmem_limit_bytes=mib << 20),
        cost_estimate=pl.CostEstimate(flops=flops, bytes_accessed=moved, transcendentals=0),
    )(*ins)


def shape(*dims, dtype=BF16):
    return jax.ShapeDtypeStruct(dims, dtype)


def lanes_of(index, width=LANES):
    return pl.ds(pl.multiple_of(index * width, LANES), width)


def rows_of(index, count):
    return pl.ds(pl.multiple_of(index * count, count), count)


def halves(block):
    half = block.shape[0] // 2
    return jnp.concatenate([block[:half], block[half:]], axis=1)


def pack_body(r, width, me, q_nope, q_rope, grad, latent, rope_t, up_keys, up_values, *refs):
    pieces, refs = refs[:H_DEV], refs[H_DEV:]
    latent_v, q_rope_v, rope_v, keys_v, values_v, sems = refs
    head_here = me[0] // r
    half = width // 2
    moves = [(latent, latent_v), (up_keys, keys_v), (up_values, values_v)]
    moves += [(rope_t, rope_v), (q_rope, q_rope_v)]
    for k in range(H_DEV):
        columns = lanes_of(head_here ^ k)
        moves.append((q_nope.at[:, columns], pieces[k].at[0:width]))
        moves.append((grad.at[:, columns], pieces[k].at[width : 2 * width]))
    copies = [pltpu.make_async_copy(a, b, sems.at[i]) for i, (a, b) in enumerate(moves)]
    for copy in copies:
        copy.start()
    for copy in copies[:5]:
        copy.wait()
    rope = halves(rope_v[...].T)
    at = 2 * width + half
    for k in range(H_DEV):
        out = pieces[k]
        head = head_here ^ k
        both = q_rope_v[:, lanes_of(head // 2)]
        mine = jnp.where(head % 2 == 0, both[:, :ROPE], both[:, ROPE:])
        out[2 * width : at] = halves(mine)
        up = jnp.concatenate([keys_v[:, lanes_of(head)], values_v[:, lanes_of(head)]], axis=1)
        made = dot(latent_v[...], up).astype(BF16)
        out[at : at + width] = made[:, :LANES]
        out[at + width : at + 2 * width] = made[:, LANES:]
        out[at + 2 * width : at + 2 * width + half] = rope
    for copy in copies[5:]:
        copy.wait()


def attend_body(n, r, width, me_ref, order, *refs):
    pieces, refs = refs[:n], refs[n:]
    kept, refs = refs[:r], refs[r:]
    dq_out, refs = refs[:H_DEV], refs[H_DEV:]
    kcat, kcat_t, vals, qcat, grads, scores, dattn, tops, acc, acc_rope, dq_t, dq_all, table = refs
    me = me_ref[0]
    groups = width // GROUP
    half = width // 2
    kv_at = 2 * width + half
    local = H_DEV * groups

    for m in range(n):
        piece = pieces[m]
        for g in range(groups):
            place = order[(me ^ m) * groups + g]
            key = piece[kv_at + g * GROUP : kv_at + (g + 1) * GROUP, :]
            packed = piece[kv_at + 2 * width : kv_at + 2 * width + half, :]
            rope = packed[:, g * ROPE : (g + 1) * ROPE]
            wide = jnp.concatenate([rope, jnp.zeros_like(rope)], axis=1)
            at = rows_of(place, GROUP)
            kcat[at, 0:LANES] = key
            kcat[at, LANES : 2 * LANES] = wide
            kcat_t[0:LANES, lanes_of(place)] = key.T
            kcat_t[LANES : 2 * LANES, lanes_of(place)] = wide.T
            first = kv_at + width + g * GROUP
            vals[at, :] = piece[first : first + GROUP, :]

    places = [order[(me ^ (k * r)) * groups + g] for k in range(H_DEV) for g in range(groups)]
    ranks = [sum((other < mine).astype(jnp.int32) for other in places) for mine in places]
    for k in range(H_DEV):
        piece = pieces[k * r]
        for g in range(groups):
            rank = ranks[k * groups + g]
            table[rank] = places[k * groups + g]
            at = rows_of(rank, GROUP)
            qcat[at, 0:LANES] = piece[g * GROUP : (g + 1) * GROUP, :]
            rope = piece[2 * width : 2 * width + half, g * ROPE : (g + 1) * ROPE]
            qcat[at, LANES : 2 * LANES] = jnp.concatenate([rope, jnp.zeros_like(rope)], axis=1)
            grads[at, :] = piece[width + g * GROUP : width + (g + 1) * GROUP, :]

    acc[...] = jnp.zeros_like(acc)
    acc_rope[...] = jnp.zeros_like(acc_rope)

    def tile(t, carry):
        q_rows = rows_of(t, TILE)
        query = qcat[q_rows, :]
        grad = grads[q_rows, :]
        first, second = table[2 * t], table[2 * t + 1]
        lane = lax.broadcasted_iota(jnp.int32, (1, TILE), 1)
        q_pos = jnp.where(lane < GROUP, first * GROUP + lane, second * GROUP + lane - GROUP)
        chunks = second // (CHUNK // GROUP) + 1

        def scan(c, carry):
            top, total, weighted = carry
            at = rows_of(c, CHUNK)
            raw = dot(kcat[at, :], query, NT)
            k_pos = c * CHUNK + lax.broadcasted_iota(jnp.int32, (CHUNK, TILE), 0)
            raw = jnp.where(k_pos <= q_pos, raw, NEG_LARGE)
            new_top = jnp.maximum(top, jnp.max(raw, axis=0, keepdims=True))
            expd = jnp.exp2((raw - new_top) * SCALE2)
            dat = dot(vals[at, :], grad, NT)
            factor = jnp.exp2((top - new_top) * SCALE2)
            scores[at, :] = expd
            dattn[at, :] = dat
            tops[pl.ds(c, 1), :] = new_top
            total = total * factor + jnp.sum(expd, axis=0, keepdims=True)
            weighted = weighted * factor + jnp.sum(expd * dat, axis=0, keepdims=True)
            return new_top, total, weighted

        start = (
            jnp.full((1, TILE), NEG_LARGE, F32),
            jnp.zeros((1, TILE), F32),
            jnp.zeros((1, TILE), F32),
        )
        top, total, weighted = lax.fori_loop(0, chunks, scan, start)
        inverse = 1.0 / total
        delta = weighted * inverse
        dq_t[...] = jnp.zeros_like(dq_t)

        def grad_step(c, carry):
            at = rows_of(c, CHUNK)
            factor = jnp.exp2((tops[pl.ds(c, 1), :] - top) * SCALE2) * inverse
            attn = scores[at, :] * factor
            dscore = (attn * (dattn[at, :] - delta)).astype(BF16)
            acc[1, at, :] += dot(attn.astype(BF16), grad)
            dk = dot(dscore, query)
            acc[0, at, :] += dk[:, 0:LANES]
            acc_rope[at, :] += dk[:, LANES : 2 * LANES]
            columns = pl.ds(pl.multiple_of(c * CHUNK, CHUNK), CHUNK)
            dq_t[...] += dot(kcat_t[:, columns], dscore)
            return carry

        lax.fori_loop(0, chunks, grad_step, 0)
        dq_all[q_rows, :] = (dq_t[...] * SCALE).T.astype(BF16)
        return carry

    lax.fori_loop(0, local // 2, tile, 0)

    for k in range(H_DEV):
        out = dq_out[k]
        ropes = []
        for g in range(groups):
            at = rows_of(ranks[k * groups + g], GROUP)
            out[g * GROUP : (g + 1) * GROUP, :] = dq_all[at, 0:LANES]
            ropes.append(dq_all[at, LANES : 2 * LANES][:, :ROPE])
        out[width : width + half, :] = jnp.concatenate(ropes, axis=1)

    unit = 2 * width + half
    for j in range(r):
        out = kept[j]
        for k in range(H_DEV):
            ropes = []
            for g in range(groups):
                at = rows_of(order[(me ^ (k * r + j)) * groups + g], GROUP)
                first = k * unit + g * GROUP
                out[first : first + GROUP, :] = (acc[0, at, :] * SCALE).astype(out.dtype)
                out[first + width : first + width + GROUP, :] = acc[1, at, :].astype(out.dtype)
                ropes.append(acc_rope[at, :][:, :ROPE])
            out[k * unit + 2 * width : (k + 1) * unit, :] = (
                jnp.concatenate(ropes, axis=1) * SCALE
            ).astype(out.dtype)


def combine_body(unit, keep, *refs):
    got, outs = refs[:-H_DEV], refs[-H_DEV:]
    for k, out in enumerate(outs):
        rows = slice(k * unit, (k + 1) * unit)
        out[...] = (keep[rows, :] + sum(x[rows, :].astype(F32) for x in got)).astype(BF16)


def weights_body(r, width, rows, me_ref, *refs):
    latents, refs = refs[:H_DEV], refs[H_DEV:]
    grads, refs = refs[:H_DEV], refs[H_DEV:]
    outs, total = refs[:r], refs[r]
    me = me_ref[0]
    value = jnp.zeros(total.shape, F32)
    for k in range(H_DEV):
        pair = jnp.concatenate([grads[k][0:width, :], grads[k][width : 2 * width, :]], axis=1)
        value += dot(latents[k][...], pair, TN)
    total[...] = value
    for j in range(r):
        for k in range(H_DEV):
            part = total[rows_of(me ^ (k * r + j), rows), :].astype(outs[j].dtype)
            first = 2 * k * rows
            outs[j][first : first + rows, :] = part[:, :LANES]
            outs[j][first + rows : first + 2 * rows, :] = part[:, LANES:]


def mix_body(unit, keep, *refs):
    dqs, refs = refs[:H_DEV], refs[H_DEV:]
    got, outs = refs[:-H_DEV], refs[-H_DEV:]
    for k, out in enumerate(outs):
        size = dqs[k].shape[0]
        rows = slice(k * unit, (k + 1) * unit)
        out[0:size, :] = dqs[k][...]
        out[size : size + unit, :] = (
            keep[rows, :] + sum(x[rows, :].astype(F32) for x in got)
        ).astype(BF16)


def latent_body(r, width, z_size, ids, *refs):
    own, refs = refs[:H_DEV], refs[H_DEV:]
    up_keys, up_values, kept, *refs = refs
    outs, (total, total_rope) = refs[: z_size - 1], refs[z_size - 1 :]
    me, z = ids[0], ids[1]
    rope = jnp.zeros((width // 2, LANES), F32)
    value = jnp.zeros(total.shape, F32)
    for k in range(H_DEV):
        head = (me // r) ^ k
        pair = jnp.concatenate([own[k][0:width, :], own[k][width : 2 * width, :]], axis=1)
        up = jnp.concatenate([up_keys[:, lanes_of(head)], up_values[:, lanes_of(head)]], axis=1)
        value += dot(pair, up, NT)
        rope += own[k][2 * width : 2 * width + width // 2, :].astype(F32)
    total[...] = value
    total_rope[...] = rope
    tokens = width // z_size
    blocks = total.shape[1] // LANES
    for k in range(z_size):
        out = kept if k == 0 else outs[k - 1]
        part = total[rows_of(z ^ k, tokens), :].astype(out.dtype)
        for i in range(blocks):
            out[i * tokens : (i + 1) * tokens, :] = part[:, i * LANES : (i + 1) * LANES]
        out[blocks * tokens :, :] = total_rope[rows_of(z ^ k, tokens // 2), :].astype(out.dtype)


def sum_body(kept, *refs):
    *got, out = refs
    out[...] = (kept[...] + sum(x[...].astype(F32) for x in got)).astype(BF16)


def finish_body(z_size, width, ids, *refs):
    parts, (grad_latent, grad_rope_t, rope) = refs[:z_size], refs[z_size:]
    z = ids[1]
    tokens = width // z_size
    blocks = grad_latent.shape[1] // LANES
    for k in range(z_size):
        part = parts[k][...].astype(F32)
        for i in range(blocks):
            grad_latent[rows_of(z ^ k, tokens), i * LANES : (i + 1) * LANES] = part[
                i * tokens : (i + 1) * tokens, :
            ]
        rope[rows_of(z ^ k, tokens // 2), :] = part[blocks * tokens :, :]
    both = rope[...].T
    grad_rope_t[:, : width // 2] = both[:ROPE, :]
    grad_rope_t[:, width // 2 :] = both[ROPE:, :]


def unpack_body(r, width, rows, me_ref, *refs):
    own, refs = refs[:H_DEV], refs[H_DEV:]
    grad_q_nope, grad_q_rope, grad_up_keys, grad_up_values = refs
    me = me_ref[0]
    at = width + width // 2
    ropes = []
    for k in range(H_DEV):
        head = (me // r) ^ k
        grad_q_nope[:, lanes_of(head)] = own[k][0:width, :]
        packed = own[k][width:at, :]
        ropes.append(jnp.concatenate([packed[:, :ROPE], packed[:, ROPE:]], axis=0))
        grad_up_keys[:, lanes_of(head)] = own[k][at : at + rows, :].astype(F32)
        grad_up_values[:, lanes_of(head)] = own[k][at + rows : at + 2 * rows, :].astype(F32)
    for k in range(0, H_DEV, 2):
        head = (me // r) ^ k
        a, b = ropes[k], ropes[k + 1]
        even = head % 2 == 0
        grad_q_rope[:, lanes_of(head // 2)] = jnp.concatenate(
            [jnp.where(even, a, b), jnp.where(even, b, a)], axis=1
        )


def per_device(q_nope, q_rope, latent, rope_keys, out_grad, up_keys, up_values, group_order):
    width = q_nope.shape[0]
    depth = latent.shape[1]
    n = lax.axis_size("ctx")
    z_size = lax.axis_size("head")
    r = n // H_DEV
    groups = width // GROUP
    half = width // 2
    seq_len = n * width
    me = lax.axis_index("ctx")
    ids = jnp.stack([me, lax.axis_index("head")]).astype(jnp.int32)
    unit = 2 * width + half
    rows = depth // n

    def over_ctx(x, mask):
        return lax.ppermute(x, "ctx", [(i, i ^ mask) for i in range(n)])

    def over_head(x, mask):
        return lax.ppermute(x, "head", [(i, i ^ mask) for i in range(z_size)])

    def across(pieces):
        return [pieces[0]] + [over_ctx(pieces[k], k * r) for k in range(1, H_DEV)]

    def shared(pieces):
        return [over_ctx(p, j) if j else p for p in pieces for j in range(r)]

    pieces = call(
        functools.partial(pack_body, r, width),
        [shape(2 * unit, LANES)] * H_DEV,
        [ids, q_nope, q_rope, out_grad, latent, rope_keys.T, up_keys, up_values],
        scratch=[
            pltpu.VMEM(latent.shape, BF16),
            pltpu.VMEM(q_rope.shape, BF16),
            pltpu.VMEM((ROPE, width), BF16),
            pltpu.VMEM(up_keys.shape, BF16),
            pltpu.VMEM(up_values.shape, BF16),
            pltpu.SemaphoreType.DMA((5 + 2 * H_DEV,)),
        ],
        flops=4 * width * depth * H_DEV * HEAD_DIM,
        hbm=True,
    )
    arrived = across(pieces)
    everyone = shared(arrived)
    later = lax.optimization_barrier((latent, everyone[1]))[0]
    latents = across([later] * H_DEV)

    queries = H_DEV * width
    outs = call(
        functools.partial(attend_body, n, r, width),
        [
            shape(H_DEV * unit, LANES, dtype=F32),
            *[shape(H_DEV * unit, LANES)] * (r - 1),
            *[shape(width + half, LANES)] * H_DEV,
        ],
        [ids, group_order, *everyone],
        scratch=[
            pltpu.VMEM((seq_len, 2 * LANES), BF16),
            pltpu.VMEM((2 * LANES, seq_len), BF16),
            pltpu.VMEM((seq_len, LANES), BF16),
            pltpu.VMEM((queries, 2 * LANES), BF16),
            pltpu.VMEM((queries, LANES), BF16),
            pltpu.VMEM((seq_len, TILE), F32),
            pltpu.VMEM((seq_len, TILE), F32),
            pltpu.VMEM((max(8, seq_len // CHUNK), TILE), F32),
            pltpu.VMEM((2, seq_len, LANES), F32),
            pltpu.VMEM((seq_len, LANES), F32),
            pltpu.VMEM((2 * LANES, TILE), F32),
            pltpu.VMEM((queries, 2 * LANES), BF16),
            pltpu.SMEM((H_DEV * groups,), jnp.int32),
        ],
        mib=40,
        flops=6 * queries * seq_len * (HEAD_DIM + ROPE + HEAD_DIM),
    )
    keep, sends, dqs = outs[0], outs[1:r], outs[r:]
    got = [over_ctx(x, j + 1) for j, x in enumerate(sends)]
    dkv = call(
        functools.partial(combine_body, unit), [shape(unit, LANES)] * H_DEV, [keep, *got], mib=24
    )
    own = across(dkv)

    keep_w, *sends_w = call(
        functools.partial(weights_body, r, width, rows),
        [shape(2 * H_DEV * rows, LANES, dtype=F32)] + [shape(2 * H_DEV * rows, LANES)] * (r - 1),
        [ids, *latents, *dkv],
        scratch=[pltpu.VMEM((depth, 2 * LANES), F32)],
        mib=24,
        flops=4 * H_DEV * width * depth * LANES,
    )
    got_w = [over_ctx(x, j + 1) for j, x in enumerate(sends_w)]
    mixed = across(
        call(
            functools.partial(mix_body, 2 * rows),
            [shape(width + half + 2 * rows, LANES)] * H_DEV,
            [keep_w, *dqs, *got_w],
        )
    )

    tokens = width // z_size
    z_rows = depth // LANES * tokens + tokens // 2
    kept, *for_planes = call(
        functools.partial(latent_body, r, width, z_size),
        [shape(z_rows, LANES, dtype=F32)] + [shape(z_rows, LANES)] * (z_size - 1),
        [ids, *own, up_keys, up_values],
        scratch=[pltpu.VMEM((width, depth), F32), pltpu.VMEM((half, LANES), F32)],
        flops=4 * width * depth * H_DEV * HEAD_DIM,
    )
    received = [over_head(x, k + 1) for k, x in enumerate(for_planes)]
    (part,) = call(sum_body, [shape(z_rows, LANES)], [kept, *received])
    parts = [part] + [over_head(part, k) for k in range(1, z_size)]
    grad_latent, grad_rope_t = call(
        functools.partial(finish_body, z_size, width),
        [shape(width, depth, dtype=F32), shape(ROPE, width, dtype=F32)],
        [ids, *parts],
        scratch=[pltpu.VMEM((half, LANES), F32)],
    )

    grad_q_nope, grad_q_rope, grad_up_keys, grad_up_values = call(
        functools.partial(unpack_body, r, width, rows),
        [
            shape(width, H_DEV * HEAD_DIM),
            shape(width, H_DEV * ROPE),
            shape(rows, H_DEV * HEAD_DIM, dtype=F32),
            shape(rows, H_DEV * HEAD_DIM, dtype=F32),
        ],
        [ids, *mixed],
    )
    return (grad_q_nope, grad_q_rope, grad_latent, grad_rope_t.T, grad_up_keys, grad_up_values)


def solution(mesh):
    in_specs = (
        P("ctx", "head"),
        P("ctx", "head"),
        P("ctx", None),
        P("ctx", None),
        P("ctx", "head"),
        P(None, "head"),
        P(None, "head"),
        P(),
    )
    out_specs = (
        P("ctx", "head"),
        P("ctx", "head"),
        P("ctx", None),
        P("ctx", None),
        P("ctx", "head"),
        P("ctx", "head"),
    )
    return jax.shard_map(
        per_device, mesh=mesh, in_specs=in_specs, out_specs=out_specs, check_vma=False
    )
```

```python
import functools
import math

import jax
import jax.numpy as jnp
from jax import lax
from jax.experimental import pallas as pl
from jax.experimental.pallas import tpu as pltpu
from jax.sharding import PartitionSpec as P

ROPE = 64
HEAD_DIM = 128
H_DEV = 4
GROUP = 128
LANES = 128
TILE = 2 * GROUP
SCALE = (HEAD_DIM + ROPE) ** (-0.5)
SCALE2 = SCALE * math.log2(math.e)
NEG_LARGE = -1e30

F32 = jnp.float32
BF16 = jnp.bfloat16
NT = (((1,), (1,)), ((), ()))
TN = (((0,), (0,)), ((), ()))
NN = (((1,), (0,)), ((), ()))
VMEM = pl.BlockSpec(memory_space=pltpu.VMEM)
SMEM = pl.BlockSpec(memory_space=pltpu.SMEM)
HBM = pl.BlockSpec(memory_space=pltpu.HBM)


def dot(a, b, dims=NN):
    return lax.dot_general(a, b, dims, preferred_element_type=F32)


def call(body, outs, ins, scratch=(), mib=16, flops=0, hbm=False):
    held = HBM if hbm else VMEM
    moved = sum(math.prod(x.shape) * x.dtype.itemsize for x in (*outs, *ins))
    return pl.pallas_call(
        body,
        out_shape=list(outs),
        in_specs=[SMEM if x.dtype == jnp.int32 else held for x in ins],
        out_specs=[VMEM] * len(outs),
        scratch_shapes=list(scratch),
        compiler_params=pltpu.CompilerParams(vmem_limit_bytes=mib << 20),
        cost_estimate=pl.CostEstimate(flops=flops, bytes_accessed=moved, transcendentals=0),
    )(*ins)


def shape(*dims, dtype=BF16):
    return jax.ShapeDtypeStruct(dims, dtype)


def lanes_of(index, width=LANES):
    return pl.ds(pl.multiple_of(index * width, LANES), width)


def rows_of(index, count):
    return pl.ds(pl.multiple_of(index * count, count), count)


def halves(block):
    half = block.shape[0] // 2
    return jnp.concatenate([block[:half], block[half:]], axis=1)


def pack_body(r, width, q_nope, q_rope, grad, latent, rope_t, up_keys, up_values, *refs):
    pieces, refs = refs[:H_DEV], refs[H_DEV:]
    latent_v, q_rope_v, rope_v, keys_v, values_v, sems = refs
    head_here = lax.axis_index("ctx") // r
    half = width // 2
    moves = [(latent, latent_v), (up_keys, keys_v), (up_values, values_v)]
    moves += [(rope_t, rope_v), (q_rope, q_rope_v)]
    for k in range(H_DEV):
        columns = lanes_of(head_here ^ k)
        moves.append((q_nope.at[:, columns], pieces[k].at[0:width]))
        moves.append((grad.at[:, columns], pieces[k].at[width : 2 * width]))
    copies = [pltpu.make_async_copy(a, b, sems.at[i]) for i, (a, b) in enumerate(moves)]
    for copy in copies:
        copy.start()
    for copy in copies[:5]:
        copy.wait()
    rope = halves(rope_v[...].T)
    at = 2 * width + half
    for k in range(H_DEV):
        out = pieces[k]
        head = head_here ^ k
        both = q_rope_v[:, lanes_of(head // 2)]
        mine = jnp.where(head % 2 == 0, both[:, :ROPE], both[:, ROPE:])
        out[2 * width : at] = halves(mine)
        up = jnp.concatenate([keys_v[:, lanes_of(head)], values_v[:, lanes_of(head)]], axis=1)
        made = dot(latent_v[...], up).astype(BF16)
        out[at : at + width] = made[:, :LANES]
        out[at + width : at + 2 * width] = made[:, LANES:]
        out[at + 2 * width : at + 2 * width + half] = rope
    for copy in copies[5:]:
        copy.wait()


def attend_body(n, r, width, order, *refs):
    pieces, refs = refs[:n], refs[n:]
    kept, refs = refs[:r], refs[r:]
    dq_out, refs = refs[:H_DEV], refs[H_DEV:]
    kcat, kcat_t, vals, qcat, grads, scores, dattn, dq_t, acc, acc_rope, dq_all, table = refs
    me = lax.axis_index("ctx")
    groups = width // GROUP
    half = width // 2
    kv_at = 2 * width + half
    local = H_DEV * groups
    seq_len = n * width
    chunk = max(TILE, seq_len // 8)
    depth = LANES + ROPE
    chunk = max(TILE, seq_len // 8)

    for m in range(n):
        piece = pieces[m]
        for g in range(groups):
            place = order[(me ^ m) * groups + g]
            key = piece[kv_at + g * GROUP : kv_at + (g + 1) * GROUP, :]
            packed = piece[kv_at + 2 * width : kv_at + 2 * width + half, :]
            rope = packed[:, g * ROPE : (g + 1) * ROPE]
            wide = jnp.concatenate([rope, jnp.zeros_like(rope)], axis=1)
            at = rows_of(place, GROUP)
            kcat[at, 0:LANES] = key
            kcat[at, LANES : 2 * LANES] = wide
            kcat_t[0:LANES, lanes_of(place)] = key.T
            kcat_t[LANES : 2 * LANES, lanes_of(place)] = wide.T
            first = kv_at + width + g * GROUP
            vals[at, :] = piece[first : first + GROUP, :]

    places = [order[(me ^ (k * r)) * groups + g] for k in range(H_DEV) for g in range(groups)]
    ranks = [sum((other < mine).astype(jnp.int32) for other in places) for mine in places]
    for k in range(H_DEV):
        piece = pieces[k * r]
        for g in range(groups):
            rank = ranks[k * groups + g]
            table[rank] = places[k * groups + g]
            at = rows_of(rank, GROUP)
            qcat[at, 0:LANES] = piece[g * GROUP : (g + 1) * GROUP, :]
            rope = piece[2 * width : 2 * width + half, g * ROPE : (g + 1) * ROPE]
            qcat[at, LANES : 2 * LANES] = jnp.concatenate([rope, jnp.zeros_like(rope)], axis=1)
            grads[at, :] = piece[width + g * GROUP : width + (g + 1) * GROUP, :]

    acc[...] = jnp.zeros_like(acc)
    acc_rope[...] = jnp.zeros_like(acc_rope)

    def tile_over(count, t, first, second):
        q_rows = rows_of(t, TILE)
        query, grad = qcat[q_rows, :], grads[q_rows, :]
        query_t, grad_t = query.T, grad.T
        lane = lax.broadcasted_iota(jnp.int32, (1, TILE), 1)
        q_pos = jnp.where(lane < GROUP, first * GROUP + lane, second * GROUP + lane - GROUP)
        spans = [slice(c * chunk, (c + 1) * chunk) for c in range(count)]

        def partial(x, how):
            return how(x.reshape(-1, 8, TILE), axis=0)

        top = jnp.full((8, TILE), NEG_LARGE, F32)
        for at in spans:
            raw = dot(kcat[at, :], query_t)
            if True:
                k_pos = at.start + lax.broadcasted_iota(jnp.int32, (chunk, TILE), 0)
                raw = jnp.where(k_pos <= q_pos, raw, NEG_LARGE)
            scores[at, :] = raw
            top = jnp.maximum(top, partial(raw, jnp.max))
        top = jnp.max(top, axis=0, keepdims=True)
        total = jnp.zeros((8, TILE), F32)
        weighted = jnp.zeros((8, TILE), F32)
        ahead = dot(vals[spans[0], :], grad_t)
        for c, at in enumerate(spans):
            dat = ahead
            if c + 1 < count:
                ahead = dot(vals[spans[c + 1], :], grad_t)
            expd = jnp.exp2((scores[at, :] - top) * SCALE2)
            scores[at, :] = expd
            dattn[at, :] = dat
            total += partial(expd, jnp.sum)
            weighted += partial(expd * dat, jnp.sum)
        inverse = 1.0 / jnp.sum(total, axis=0, keepdims=True)
        delta = jnp.sum(weighted, axis=0, keepdims=True) * inverse

        def weigh(at):
            attn = scores[at, :] * inverse
            return attn.astype(BF16), (attn * (dattn[at, :] - delta)).astype(BF16)

        ahead = weigh(spans[0])
        for c, at in enumerate(spans):
            attn, dscore = ahead
            if c + 1 < count:
                ahead = weigh(spans[c + 1])
            acc[1, at, :] += dot(attn, grad)
            dk = dot(dscore, query)
            acc[0, at, :] += dk[:, 0:LANES]
            acc_rope[at, 0:ROPE] += dk[:, LANES : LANES + ROPE]
            if at.start == 0:
                dq_t[0:depth, :] = dot(kcat_t[0:depth, at], dscore)
            else:
                dq_t[0:depth, :] += dot(kcat_t[0:depth, at], dscore)
        dq_all[q_rows, :] = (dq_t[...] * SCALE).T.astype(BF16)

    def tile(t, carry):
        first, second = table[2 * t], table[2 * t + 1]
        need = second // (chunk // GROUP) + 1
        for count in range(1, seq_len // chunk + 1):
            pl.when(need == count)(functools.partial(tile_over, count, t, first, second))
        return carry

    lax.fori_loop(0, local // 2, tile, 0)

    for k in range(H_DEV):
        out = dq_out[k]
        ropes = []
        for g in range(groups):
            at = rows_of(ranks[k * groups + g], GROUP)
            out[g * GROUP : (g + 1) * GROUP, :] = dq_all[at, 0:LANES]
            ropes.append(dq_all[at, LANES : 2 * LANES][:, :ROPE])
        out[width : width + half, :] = jnp.concatenate(ropes, axis=1)

    unit = 2 * width + half
    for j in range(r):
        out = kept[j]
        for k in range(H_DEV):
            ropes = []
            for g in range(groups):
                at = rows_of(order[(me ^ (k * r + j)) * groups + g], GROUP)
                first = k * unit + g * GROUP
                out[first : first + GROUP, :] = (acc[0, at, :] * SCALE).astype(out.dtype)
                out[first + width : first + width + GROUP, :] = acc[1, at, :].astype(out.dtype)
                ropes.append(acc_rope[at, :][:, :ROPE])
            out[k * unit + 2 * width : (k + 1) * unit, :] = (
                jnp.concatenate(ropes, axis=1) * SCALE
            ).astype(out.dtype)


def combine_body(unit, keep, *refs):
    got, outs = refs[:-H_DEV], refs[-H_DEV:]
    for k, out in enumerate(outs):
        rows = slice(k * unit, (k + 1) * unit)
        out[...] = (keep[rows, :] + sum(x[rows, :].astype(F32) for x in got)).astype(BF16)


def weights_body(r, width, rows, *refs):
    latents, refs = refs[:H_DEV], refs[H_DEV:]
    grads, refs = refs[:H_DEV], refs[H_DEV:]
    outs, total = refs[:r], refs[r]
    me = lax.axis_index("ctx")
    value = jnp.zeros(total.shape, F32)
    for k in range(H_DEV):
        pair = jnp.concatenate([grads[k][0:width, :], grads[k][width : 2 * width, :]], axis=1)
        value += dot(latents[k][...], pair, TN)
    total[...] = value
    for j in range(r):
        for k in range(H_DEV):
            part = total[rows_of(me ^ (k * r + j), rows), :].astype(outs[j].dtype)
            first = 2 * k * rows
            outs[j][first : first + rows, :] = part[:, :LANES]
            outs[j][first + rows : first + 2 * rows, :] = part[:, LANES:]


def mix_body(unit, keep, *refs):
    dqs, refs = refs[:H_DEV], refs[H_DEV:]
    got, outs = refs[:-H_DEV], refs[-H_DEV:]
    for k, out in enumerate(outs):
        size = dqs[k].shape[0]
        rows = slice(k * unit, (k + 1) * unit)
        out[0:size, :] = dqs[k][...]
        value = keep[rows, :] + sum(x[rows, :].astype(F32) for x in got)
        out[size : size + unit, :] = value.astype(BF16)


def latent_body(r, width, z_size, *refs):
    own, refs = refs[:H_DEV], refs[H_DEV:]
    up_keys, up_values, kept, *refs = refs
    outs, (total, total_rope) = refs[: z_size - 1], refs[z_size - 1 :]
    me, z = lax.axis_index("ctx"), lax.axis_index("head")
    rope = jnp.zeros((width // 2, LANES), F32)
    value = jnp.zeros(total.shape, F32)
    for k in range(H_DEV):
        head = (me // r) ^ k
        pair = jnp.concatenate([own[k][0:width, :], own[k][width : 2 * width, :]], axis=1)
        up = jnp.concatenate([up_keys[:, lanes_of(head)], up_values[:, lanes_of(head)]], axis=1)
        value += dot(pair, up, NT)
        rope += own[k][2 * width : 2 * width + width // 2, :].astype(F32)
    total[...] = value
    total_rope[...] = rope
    tokens = width // z_size
    blocks = total.shape[1] // LANES
    for k in range(z_size):
        out = kept if k == 0 else outs[k - 1]
        part = total[rows_of(z ^ k, tokens), :].astype(out.dtype)
        for i in range(blocks):
            out[i * tokens : (i + 1) * tokens, :] = part[:, i * LANES : (i + 1) * LANES]
        out[blocks * tokens :, :] = total_rope[rows_of(z ^ k, tokens // 2), :].astype(out.dtype)


def sum_body(kept, *refs):
    *got, out = refs
    out[...] = (kept[...] + sum(x[...].astype(F32) for x in got)).astype(BF16)


def finish_body(z_size, width, *refs):
    parts, (grad_latent, grad_rope_t, rope) = refs[:z_size], refs[z_size:]
    z = lax.axis_index("head")
    tokens = width // z_size
    blocks = grad_latent.shape[1] // LANES
    for k in range(z_size):
        part = parts[k][...].astype(F32)
        for i in range(blocks):
            grad_latent[rows_of(z ^ k, tokens), i * LANES : (i + 1) * LANES] = part[
                i * tokens : (i + 1) * tokens, :
            ]
        rope[rows_of(z ^ k, tokens // 2), :] = part[blocks * tokens :, :]
    both = rope[...].T
    grad_rope_t[:, : width // 2] = both[:ROPE, :]
    grad_rope_t[:, width // 2 :] = both[ROPE:, :]


def unpack_body(r, width, rows, *refs):
    own, refs = refs[:H_DEV], refs[H_DEV:]
    grad_q_nope, grad_q_rope, grad_up_keys, grad_up_values = refs
    me = lax.axis_index("ctx")
    first = width + width // 2
    ropes = []
    for k in range(H_DEV):
        head = (me // r) ^ k
        grad_q_nope[:, lanes_of(head)] = own[k][0:width, :]
        packed = own[k][width:first, :]
        ropes.append(jnp.concatenate([packed[:, :ROPE], packed[:, ROPE:]], axis=0))
        grad_up_keys[:, lanes_of(head)] = own[k][first : first + rows, :].astype(F32)
        grad_up_values[:, lanes_of(head)] = own[k][first + rows : first + 2 * rows, :].astype(F32)
    for k in range(0, H_DEV, 2):
        head = (me // r) ^ k
        a, b = ropes[k], ropes[k + 1]
        even = head % 2 == 0
        grad_q_rope[:, lanes_of(head // 2)] = jnp.concatenate(
            [jnp.where(even, a, b), jnp.where(even, b, a)], axis=1
        )


def attend(n, r, width, group_order, everyone):
    seq_len = n * width
    half = width // 2
    groups = width // GROUP
    unit = 2 * width + half
    queries = H_DEV * width
    return call(
        functools.partial(attend_body, n, r, width),
        [
            shape(H_DEV * unit, LANES, dtype=F32),
            *[shape(H_DEV * unit, LANES)] * (r - 1),
            *[shape(width + half, LANES)] * H_DEV,
        ],
        [group_order, *everyone],
        scratch=[
            pltpu.VMEM((seq_len, 2 * LANES), BF16),
            pltpu.VMEM((2 * LANES, seq_len), BF16),
            pltpu.VMEM((seq_len, LANES), BF16),
            pltpu.VMEM((queries, 2 * LANES), BF16),
            pltpu.VMEM((queries, LANES), BF16),
            pltpu.VMEM((seq_len, TILE), F32),
            pltpu.VMEM((seq_len, TILE), F32),
            pltpu.VMEM((2 * LANES, TILE), F32),
            pltpu.VMEM((2, seq_len, LANES), F32),
            pltpu.VMEM((seq_len, LANES), F32),
            pltpu.VMEM((queries, 2 * LANES), BF16),
            pltpu.SMEM((H_DEV * groups,), jnp.int32),
        ],
        mib=40,
    )


def per_device(q_nope, q_rope, latent, rope_keys, out_grad, up_keys, up_values, group_order):
    width = q_nope.shape[0]
    depth = latent.shape[1]
    n = lax.axis_size("ctx")
    z_size = lax.axis_size("head")
    r = n // H_DEV
    half = width // 2
    unit = 2 * width + half
    rows = depth // n

    def over_ctx(x, mask):
        return lax.ppermute(x, "ctx", [(i, i ^ mask) for i in range(n)])

    def over_head(x, mask):
        return lax.ppermute(x, "head", [(i, i ^ mask) for i in range(z_size)])

    def across(pieces):
        return [pieces[0]] + [over_ctx(pieces[k], k * r) for k in range(1, H_DEV)]

    def shared(pieces):
        return [over_ctx(p, j) if j else p for p in pieces for j in range(r)]

    def combine(size, parts, mib=16):
        got = [over_ctx(x, j + 1) for j, x in enumerate(parts[1:])]
        return call(
            functools.partial(combine_body, size),
            [shape(size, LANES)] * H_DEV,
            [parts[0], *got],
            mib=mib,
        )

    pieces = call(
        functools.partial(pack_body, r, width),
        [shape(2 * unit, LANES)] * H_DEV,
        [q_nope, q_rope, out_grad, latent, rope_keys.T, up_keys, up_values],
        scratch=[
            pltpu.VMEM(latent.shape, BF16),
            pltpu.VMEM(q_rope.shape, BF16),
            pltpu.VMEM((ROPE, width), BF16),
            pltpu.VMEM(up_keys.shape, BF16),
            pltpu.VMEM(up_values.shape, BF16),
            pltpu.SemaphoreType.DMA((5 + 2 * H_DEV,)),
        ],
        flops=4 * width * depth * H_DEV * HEAD_DIM,
        mib=60,
        hbm=True,
    )
    arrived = across(pieces)
    latents = across([latent] * H_DEV)
    everyone = shared(arrived)
    outs = attend(n, r, width, group_order, everyone)
    dqs = outs[r:]
    outs, latents = lax.optimization_barrier((outs[:r], latents))
    dkv = combine(unit, outs[:r], mib=24)
    own = across(dkv)

    unit_w = 2 * rows
    parts = call(
        functools.partial(weights_body, r, width, rows),
        [shape(H_DEV * unit_w, LANES, dtype=F32)] + [shape(H_DEV * unit_w, LANES)] * (r - 1),
        [*latents, *dkv],
        scratch=[pltpu.VMEM((depth, 2 * LANES), F32)],
        mib=24,
        flops=4 * H_DEV * width * depth * LANES,
    )
    got = [over_ctx(x, j + 1) for j, x in enumerate(parts[1:])]
    ready = call(
        functools.partial(mix_body, unit_w),
        [shape(width + half + unit_w, LANES)] * H_DEV,
        [parts[0], *dqs, *got],
    )
    mixed = across(ready)
    up_keys = lax.optimization_barrier((up_keys, ready))[0]

    tokens = width // z_size
    z_rows = depth // LANES * tokens + tokens // 2
    kept, *for_planes = call(
        functools.partial(latent_body, r, width, z_size),
        [shape(z_rows, LANES, dtype=F32)] + [shape(z_rows, LANES)] * (z_size - 1),
        [*own, up_keys, up_values],
        scratch=[pltpu.VMEM((width, depth), F32), pltpu.VMEM((half, LANES), F32)],
        flops=4 * width * depth * H_DEV * HEAD_DIM,
    )
    received = [over_head(x, k + 1) for k, x in enumerate(for_planes)]
    (part,) = call(sum_body, [shape(z_rows, LANES)], [kept, *received])
    parts = [part] + [over_head(part, k) for k in range(1, z_size)]
    grad_latent, grad_rope_t = call(
        functools.partial(finish_body, z_size, width),
        [shape(width, depth, dtype=F32), shape(ROPE, width, dtype=F32)],
        parts,
        scratch=[pltpu.VMEM((half, LANES), F32)],
    )

    grad_q_nope, grad_q_rope, grad_up_keys, grad_up_values = call(
        functools.partial(unpack_body, r, width, rows),
        [
            shape(width, H_DEV * HEAD_DIM),
            shape(width, H_DEV * ROPE),
            shape(rows, H_DEV * HEAD_DIM, dtype=F32),
            shape(rows, H_DEV * HEAD_DIM, dtype=F32),
        ],
        mixed,
    )
    return (grad_q_nope, grad_q_rope, grad_latent, grad_rope_t.T, grad_up_keys, grad_up_values)


def solution(mesh):
    in_specs = (
        P("ctx", "head"),
        P("ctx", "head"),
        P("ctx", None),
        P("ctx", None),
        P("ctx", "head"),
        P(None, "head"),
        P(None, "head"),
        P(),
    )
    out_specs = (
        P("ctx", "head"),
        P("ctx", "head"),
        P("ctx", None),
        P("ctx", None),
        P("ctx", "head"),
        P("ctx", "head"),
    )
    return jax.shard_map(
        per_device, mesh=mesh, in_specs=in_specs, out_specs=out_specs, check_vma=False
    )
```

```python
import functools
import math

import jax
import jax.numpy as jnp
from jax import lax
from jax.experimental import pallas as pl
from jax.experimental.pallas import tpu as pltpu
from jax.sharding import PartitionSpec as P

ROPE = 64
HEAD_DIM = 128
H_DEV = 4
GROUP = 128
LANES = 128
TILE = 2 * GROUP
SCALE = (HEAD_DIM + ROPE) ** (-0.5)
SCALE2 = SCALE * math.log2(math.e)
NEG_LARGE = -1e30

F32 = jnp.float32
BF16 = jnp.bfloat16
NT = (((1,), (1,)), ((), ()))
TN = (((0,), (0,)), ((), ()))
NN = (((1,), (0,)), ((), ()))
VMEM = pl.BlockSpec(memory_space=pltpu.VMEM)
SMEM = pl.BlockSpec(memory_space=pltpu.SMEM)
HBM = pl.BlockSpec(memory_space=pltpu.HBM)


def dot(a, b, dims=NN):
    return lax.dot_general(a, b, dims, preferred_element_type=F32)


def call(body, outs, ins, scratch=(), mib=16, hbm=False):
    held = HBM if hbm else VMEM
    return pl.pallas_call(
        body,
        out_shape=list(outs),
        in_specs=[SMEM if x.dtype == jnp.int32 else held for x in ins],
        out_specs=[VMEM] * len(outs),
        scratch_shapes=list(scratch),
        compiler_params=pltpu.CompilerParams(vmem_limit_bytes=int(mib * 2**20)),
        cost_estimate=pl.CostEstimate(flops=0, bytes_accessed=0, transcendentals=0),
    )(*ins)


def shape(*dims, dtype=BF16):
    return jax.ShapeDtypeStruct(dims, dtype)


def lanes_of(index, width=LANES):
    return pl.ds(pl.multiple_of(index * width, LANES), width)


def rows_of(index, count):
    return pl.ds(pl.multiple_of(index * count, count), count)


def halves(block):
    half = block.shape[0] // 2
    return jnp.concatenate([block[:half], block[half:]], axis=1)


def keys_body(r, width, latent, rope_t, up_keys, up_values, *refs):
    keys, refs = refs[:H_DEV], refs[H_DEV:]
    latent_v, rope_v, keys_v, values_v, sems = refs
    head_here = lax.axis_index("ctx") // r
    half = width // 2
    moves = [(latent, latent_v), (up_keys, keys_v), (up_values, values_v), (rope_t, rope_v)]
    copies = [pltpu.make_async_copy(a, b, sems.at[i]) for i, (a, b) in enumerate(moves)]
    for copy in copies:
        copy.start()
    for copy in copies:
        copy.wait()
    rope = halves(rope_v[...].T)
    for k in range(H_DEV):
        columns = lanes_of(head_here ^ k)
        up = jnp.concatenate([keys_v[:, columns], values_v[:, columns]], axis=1)
        made = dot(latent_v[...], up).astype(BF16)
        keys[k][0:width] = made[:, :LANES]
        keys[k][width : 2 * width] = made[:, LANES:]
        keys[k][2 * width : 2 * width + half] = rope


def queries_body(r, width, q_nope, q_rope, grad, *queries):
    half = width // 2
    for k in range(H_DEV):
        head = (lax.axis_index("ctx") // r) ^ k
        columns = lanes_of(head)
        queries[k][0:width] = q_nope[:, columns]
        queries[k][width : 2 * width] = grad[:, columns]
        both = q_rope[:, lanes_of(head // 2)]
        mine = jnp.where(head % 2 == 0, both[:, :ROPE], both[:, ROPE:])
        queries[k][2 * width : 2 * width + half] = halves(mine)


def attend_body(n, r, width, order, *refs):
    queries, refs = refs[:H_DEV], refs[H_DEV:]
    pieces, refs = refs[:n], refs[n:]
    kept, refs = refs[:r], refs[r:]
    dq_out, refs = refs[:H_DEV], refs[H_DEV:]
    kcat, kcat_t, vals, qcat, grads, scores, dattn, dq_t, acc, acc_rope, dq_all, table = refs
    me = lax.axis_index("ctx")
    groups = width // GROUP
    half = width // 2
    local = H_DEV * groups
    seq_len = n * width
    chunk = max(TILE, seq_len // 8)
    depth = LANES + ROPE
    chunk = max(TILE, seq_len // 8)

    for m in range(n):
        piece = pieces[m]
        for g in range(groups):
            place = order[(me ^ m) * groups + g]
            key = piece[g * GROUP : (g + 1) * GROUP, :]
            packed = piece[2 * width : 2 * width + half, :]
            rope = packed[:, g * ROPE : (g + 1) * ROPE]
            wide = jnp.concatenate([rope, jnp.zeros_like(rope)], axis=1)
            at = rows_of(place, GROUP)
            kcat[at, 0:LANES] = key
            kcat[at, LANES : 2 * LANES] = wide
            kcat_t[0:LANES, lanes_of(place)] = key.T
            kcat_t[LANES : 2 * LANES, lanes_of(place)] = wide.T
            first = width + g * GROUP
            vals[at, :] = piece[first : first + GROUP, :]

    places = [order[(me ^ (k * r)) * groups + g] for k in range(H_DEV) for g in range(groups)]
    ranks = [sum((other < mine).astype(jnp.int32) for other in places) for mine in places]
    for k in range(H_DEV):
        piece = queries[k]
        for g in range(groups):
            rank = ranks[k * groups + g]
            table[rank] = places[k * groups + g]
            at = rows_of(rank, GROUP)
            qcat[at, 0:LANES] = piece[g * GROUP : (g + 1) * GROUP, :]
            rope = piece[2 * width : 2 * width + half, g * ROPE : (g + 1) * ROPE]
            qcat[at, LANES : 2 * LANES] = jnp.concatenate([rope, jnp.zeros_like(rope)], axis=1)
            grads[at, :] = piece[width + g * GROUP : width + (g + 1) * GROUP, :]

    acc[...] = jnp.zeros_like(acc)
    acc_rope[...] = jnp.zeros_like(acc_rope)

    def tile_over(count, t, first, second):
        q_rows = rows_of(t, TILE)
        query, grad = qcat[q_rows, :], grads[q_rows, :]
        query_t, grad_t = query.T, grad.T
        lane = lax.broadcasted_iota(jnp.int32, (1, TILE), 1)
        q_pos = jnp.where(lane < GROUP, first * GROUP + lane, second * GROUP + lane - GROUP)
        spans = [slice(c * chunk, (c + 1) * chunk) for c in range(count)]

        def partial(x, how):
            return how(x.reshape(-1, 8, TILE), axis=0)

        top = jnp.full((8, TILE), NEG_LARGE, F32)
        for at in spans:
            raw = dot(kcat[at, :], query_t)
            if True:
                k_pos = at.start + lax.broadcasted_iota(jnp.int32, (chunk, TILE), 0)
                raw = jnp.where(k_pos <= q_pos, raw, NEG_LARGE)
            scores[at, :] = raw
            top = jnp.maximum(top, partial(raw, jnp.max))
        top = jnp.max(top, axis=0, keepdims=True)
        total = jnp.zeros((8, TILE), F32)
        weighted = jnp.zeros((8, TILE), F32)
        ahead = dot(vals[spans[0], :], grad_t)
        for c, at in enumerate(spans):
            dat = ahead
            if c + 1 < count:
                ahead = dot(vals[spans[c + 1], :], grad_t)
            expd = jnp.exp2((scores[at, :] - top) * SCALE2)
            scores[at, :] = expd
            dattn[at, :] = dat
            total += partial(expd, jnp.sum)
            weighted += partial(expd * dat, jnp.sum)
        inverse = 1.0 / jnp.sum(total, axis=0, keepdims=True)
        delta = jnp.sum(weighted, axis=0, keepdims=True) * inverse

        def weigh(at):
            attn = scores[at, :] * inverse
            return attn.astype(BF16), (attn * (dattn[at, :] - delta)).astype(BF16)

        ahead = weigh(spans[0])
        for c, at in enumerate(spans):
            attn, dscore = ahead
            if c + 1 < count:
                ahead = weigh(spans[c + 1])
            acc[1, at, :] += dot(attn, grad)
            dk = dot(dscore, query)
            acc[0, at, :] += dk[:, 0:LANES]
            acc_rope[at, 0:ROPE] += dk[:, LANES : LANES + ROPE]
            if at.start == 0:
                dq_t[0:depth, :] = dot(kcat_t[0:depth, at], dscore)
            else:
                dq_t[0:depth, :] += dot(kcat_t[0:depth, at], dscore)
        dq_all[q_rows, :] = (dq_t[...] * SCALE).T.astype(BF16)

    def tile(t, carry):
        first, second = table[2 * t], table[2 * t + 1]
        need = second // (chunk // GROUP) + 1
        for count in range(1, seq_len // chunk + 1):
            pl.when(need == count)(functools.partial(tile_over, count, t, first, second))
        return carry

    lax.fori_loop(0, local // 2, tile, 0)

    for k in range(H_DEV):
        out = dq_out[k]
        ropes = []
        for g in range(groups):
            at = rows_of(ranks[k * groups + g], GROUP)
            out[g * GROUP : (g + 1) * GROUP, :] = dq_all[at, 0:LANES]
            ropes.append(dq_all[at, LANES : 2 * LANES][:, :ROPE])
        out[width : width + half, :] = jnp.concatenate(ropes, axis=1)

    unit = 2 * width + half
    for j in range(r):
        out = kept[j]
        for k in range(H_DEV):
            ropes = []
            for g in range(groups):
                at = rows_of(order[(me ^ (k * r + j)) * groups + g], GROUP)
                first = k * unit + g * GROUP
                out[first : first + GROUP, :] = (acc[0, at, :] * SCALE).astype(out.dtype)
                out[first + width : first + width + GROUP, :] = acc[1, at, :].astype(out.dtype)
                ropes.append(acc_rope[at, :][:, :ROPE])
            out[k * unit + 2 * width : (k + 1) * unit, :] = (
                jnp.concatenate(ropes, axis=1) * SCALE
            ).astype(out.dtype)


def combine_body(unit, keep, *refs):
    got, outs = refs[:-H_DEV], refs[-H_DEV:]
    for k, out in enumerate(outs):
        rows = slice(k * unit, (k + 1) * unit)
        out[...] = (keep[rows, :] + sum(x[rows, :].astype(F32) for x in got)).astype(BF16)


def weights_body(r, width, rows, *refs):
    latents, refs = refs[:H_DEV], refs[H_DEV:]
    grads, refs = refs[:H_DEV], refs[H_DEV:]
    outs, total = refs[:r], refs[r]
    me = lax.axis_index("ctx")
    value = jnp.zeros(total.shape, F32)
    for k in range(H_DEV):
        pair = jnp.concatenate([grads[k][0:width, :], grads[k][width : 2 * width, :]], axis=1)
        value += dot(latents[k][...], pair, TN)
    total[...] = value
    for j in range(r):
        for k in range(H_DEV):
            part = total[rows_of(me ^ (k * r + j), rows), :].astype(outs[j].dtype)
            first = 2 * k * rows
            outs[j][first : first + rows, :] = part[:, :LANES]
            outs[j][first + rows : first + 2 * rows, :] = part[:, LANES:]


def mix_body(unit, keep, *refs):
    dqs, refs = refs[:H_DEV], refs[H_DEV:]
    got, outs = refs[:-H_DEV], refs[-H_DEV:]
    for k, out in enumerate(outs):
        size = dqs[k].shape[0]
        rows = slice(k * unit, (k + 1) * unit)
        out[0:size, :] = dqs[k][...]
        value = keep[rows, :] + sum(x[rows, :].astype(F32) for x in got)
        out[size : size + unit, :] = value.astype(BF16)


def latent_body(r, width, z_size, *refs):
    own, refs = refs[:H_DEV], refs[H_DEV:]
    up_keys, up_values, kept, *refs = refs
    outs, (total, total_rope) = refs[: z_size - 1], refs[z_size - 1 :]
    me, z = lax.axis_index("ctx"), lax.axis_index("head")
    rope = jnp.zeros((width // 2, LANES), F32)
    value = jnp.zeros(total.shape, F32)
    for k in range(H_DEV):
        head = (me // r) ^ k
        pair = jnp.concatenate([own[k][0:width, :], own[k][width : 2 * width, :]], axis=1)
        up = jnp.concatenate([up_keys[:, lanes_of(head)], up_values[:, lanes_of(head)]], axis=1)
        value += dot(pair, up, NT)
        rope += own[k][2 * width : 2 * width + width // 2, :].astype(F32)
    total[...] = value
    total_rope[...] = rope
    tokens = width // z_size
    blocks = total.shape[1] // LANES
    for k in range(z_size):
        out = kept if k == 0 else outs[k - 1]
        part = total[rows_of(z ^ k, tokens), :].astype(out.dtype)
        for i in range(blocks):
            out[i * tokens : (i + 1) * tokens, :] = part[:, i * LANES : (i + 1) * LANES]
        out[blocks * tokens :, :] = total_rope[rows_of(z ^ k, tokens // 2), :].astype(out.dtype)


def sum_body(kept, *refs):
    *got, out = refs
    out[...] = (kept[...] + sum(x[...].astype(F32) for x in got)).astype(BF16)


def finish_body(z_size, width, *refs):
    parts, (grad_latent, grad_rope_t, rope) = refs[:z_size], refs[z_size:]
    z = lax.axis_index("head")
    tokens = width // z_size
    blocks = grad_latent.shape[1] // LANES
    for k in range(z_size):
        part = parts[k][...].astype(F32)
        for i in range(blocks):
            grad_latent[rows_of(z ^ k, tokens), i * LANES : (i + 1) * LANES] = part[
                i * tokens : (i + 1) * tokens, :
            ]
        rope[rows_of(z ^ k, tokens // 2), :] = part[blocks * tokens :, :]
    both = rope[...].T
    grad_rope_t[:, : width // 2] = both[:ROPE, :]
    grad_rope_t[:, width // 2 :] = both[ROPE:, :]


def unpack_body(r, width, rows, *refs):
    own, refs = refs[:H_DEV], refs[H_DEV:]
    grad_q_nope, grad_q_rope, grad_up_keys, grad_up_values = refs
    me = lax.axis_index("ctx")
    first = width + width // 2
    ropes = []
    for k in range(H_DEV):
        head = (me // r) ^ k
        grad_q_nope[:, lanes_of(head)] = own[k][0:width, :]
        packed = own[k][width:first, :]
        ropes.append(jnp.concatenate([packed[:, :ROPE], packed[:, ROPE:]], axis=0))
        grad_up_keys[:, lanes_of(head)] = own[k][first : first + rows, :].astype(F32)
        grad_up_values[:, lanes_of(head)] = own[k][first + rows : first + 2 * rows, :].astype(F32)
    for k in range(0, H_DEV, 2):
        head = (me // r) ^ k
        a, b = ropes[k], ropes[k + 1]
        even = head % 2 == 0
        grad_q_rope[:, lanes_of(head // 2)] = jnp.concatenate(
            [jnp.where(even, a, b), jnp.where(even, b, a)], axis=1
        )


def attend(n, r, width, group_order, queries, everyone):
    seq_len = n * width
    half = width // 2
    groups = width // GROUP
    unit = 2 * width + half
    rows = H_DEV * width
    return call(
        functools.partial(attend_body, n, r, width),
        [
            shape(H_DEV * unit, LANES, dtype=F32),
            *[shape(H_DEV * unit, LANES)] * (r - 1),
            *[shape(width + half, LANES)] * H_DEV,
        ],
        [group_order, *queries, *everyone],
        scratch=[
            pltpu.VMEM((seq_len, 2 * LANES), BF16),
            pltpu.VMEM((2 * LANES, seq_len), BF16),
            pltpu.VMEM((seq_len, LANES), BF16),
            pltpu.VMEM((rows, 2 * LANES), BF16),
            pltpu.VMEM((rows, LANES), BF16),
            pltpu.VMEM((seq_len, TILE), F32),
            pltpu.VMEM((seq_len, TILE), F32),
            pltpu.VMEM((2 * LANES, TILE), F32),
            pltpu.VMEM((2, seq_len, LANES), F32),
            pltpu.VMEM((seq_len, LANES), F32),
            pltpu.VMEM((rows, 2 * LANES), BF16),
            pltpu.SMEM((H_DEV * groups,), jnp.int32),
        ],
        mib=40,
    )


def per_device(q_nope, q_rope, latent, rope_keys, out_grad, up_keys, up_values, group_order):
    width = q_nope.shape[0]
    depth = latent.shape[1]
    n = lax.axis_size("ctx")
    z_size = lax.axis_size("head")
    r = n // H_DEV
    half = width // 2
    unit = 2 * width + half
    rows = depth // n

    def over_ctx(x, mask):
        return lax.ppermute(x, "ctx", [(i, i ^ mask) for i in range(n)])

    def over_head(x, mask):
        return lax.ppermute(x, "head", [(i, i ^ mask) for i in range(z_size)])

    def across(pieces):
        return [pieces[0]] + [over_ctx(pieces[k], k * r) for k in range(1, H_DEV)]

    def shared(pieces):
        return [over_ctx(p, j) if j else p for p in pieces for j in range(r)]

    def combine(size, parts, mib=16):
        got = [over_ctx(x, j + 1) for j, x in enumerate(parts[1:])]
        return call(
            functools.partial(combine_body, size),
            [shape(size, LANES)] * H_DEV,
            [parts[0], *got],
            mib=mib,
        )

    keys = call(
        functools.partial(keys_body, r, width),
        [shape(unit, LANES)] * H_DEV,
        [latent, rope_keys.T, up_keys, up_values],
        scratch=[
            pltpu.VMEM(latent.shape, BF16),
            pltpu.VMEM((ROPE, width), BF16),
            pltpu.VMEM(up_keys.shape, BF16),
            pltpu.VMEM(up_values.shape, BF16),
            pltpu.SemaphoreType.DMA((4,)),
        ],
        mib=53.1,
        hbm=True,
    )
    queries = call(
        functools.partial(queries_body, r, width),
        [shape(unit, LANES)] * H_DEV,
        [q_nope, q_rope, out_grad],
    )
    arrived = across(keys)
    everyone = shared(arrived)
    queries = across(queries)
    latents = across([latent] * H_DEV)
    outs = attend(n, r, width, group_order, queries, everyone)
    dqs = outs[r:]
    outs, latents = lax.optimization_barrier((outs[:r], latents))
    dkv = combine(unit, outs[:r], mib=24)
    own = across(dkv)

    unit_w = 2 * rows
    parts = call(
        functools.partial(weights_body, r, width, rows),
        [shape(H_DEV * unit_w, LANES, dtype=F32)] + [shape(H_DEV * unit_w, LANES)] * (r - 1),
        [*latents, *dkv],
        scratch=[pltpu.VMEM((depth, 2 * LANES), F32)],
        mib=24,
    )
    got = [over_ctx(x, j + 1) for j, x in enumerate(parts[1:])]
    ready = call(
        functools.partial(mix_body, unit_w),
        [shape(width + half + unit_w, LANES)] * H_DEV,
        [parts[0], *dqs, *got],
    )
    mixed = across(ready)
    up_keys = lax.optimization_barrier((up_keys, ready))[0]

    tokens = width // z_size
    z_rows = depth // LANES * tokens + tokens // 2
    kept, *for_planes = call(
        functools.partial(latent_body, r, width, z_size),
        [shape(z_rows, LANES, dtype=F32)] + [shape(z_rows, LANES)] * (z_size - 1),
        [*own, up_keys, up_values],
        scratch=[pltpu.VMEM((width, depth), F32), pltpu.VMEM((half, LANES), F32)],
    )
    received = [over_head(x, k + 1) for k, x in enumerate(for_planes)]
    (part,) = call(sum_body, [shape(z_rows, LANES)], [kept, *received])
    parts = [part] + [over_head(part, k) for k in range(1, z_size)]
    grad_latent, grad_rope_t = call(
        functools.partial(finish_body, z_size, width),
        [shape(width, depth, dtype=F32), shape(ROPE, width, dtype=F32)],
        parts,
        scratch=[pltpu.VMEM((half, LANES), F32)],
    )

    grad_q_nope, grad_q_rope, grad_up_keys, grad_up_values = call(
        functools.partial(unpack_body, r, width, rows),
        [
            shape(width, H_DEV * HEAD_DIM),
            shape(width, H_DEV * ROPE),
            shape(rows, H_DEV * HEAD_DIM, dtype=F32),
            shape(rows, H_DEV * HEAD_DIM, dtype=F32),
        ],
        mixed,
    )
    return (grad_q_nope, grad_q_rope, grad_latent, grad_rope_t.T, grad_up_keys, grad_up_values)


def solution(mesh):
    in_specs = (
        P("ctx", "head"),
        P("ctx", "head"),
        P("ctx", None),
        P("ctx", None),
        P("ctx", "head"),
        P(None, "head"),
        P(None, "head"),
        P(),
    )
    out_specs = (
        P("ctx", "head"),
        P("ctx", "head"),
        P("ctx", None),
        P("ctx", None),
        P("ctx", "head"),
        P("ctx", "head"),
    )
    return jax.shard_map(
        per_device, mesh=mesh, in_specs=in_specs, out_specs=out_specs, check_vma=False
    )
```

```python
import functools
import math

import jax
import jax.numpy as jnp
from jax import lax
from jax.experimental import pallas as pl
from jax.experimental.pallas import tpu as pltpu
from jax.sharding import PartitionSpec as P

ROPE = 64
HEAD_DIM = 128
H_DEV = 4
GROUP = 128
LANES = 128
TILE = 4 * GROUP
SCALE = (HEAD_DIM + ROPE) ** (-0.5)
SCALE2 = SCALE * math.log2(math.e)
NEG_LARGE = -1e30

F32 = jnp.float32
BF16 = jnp.bfloat16
NT = (((1,), (1,)), ((), ()))
TN = (((0,), (0,)), ((), ()))
NN = (((1,), (0,)), ((), ()))
VMEM = pl.BlockSpec(memory_space=pltpu.VMEM)
SMEM = pl.BlockSpec(memory_space=pltpu.SMEM)
HBM = pl.BlockSpec(memory_space=pltpu.HBM)


def dot(a, b, dims=NN):
    return lax.dot_general(a, b, dims, preferred_element_type=F32)


def call(body, outs, ins, scratch=(), mib=16, hbm=False):
    held = HBM if hbm else VMEM
    return pl.pallas_call(
        body,
        out_shape=list(outs),
        in_specs=[SMEM if x.dtype == jnp.int32 else held for x in ins],
        out_specs=[VMEM] * len(outs),
        scratch_shapes=list(scratch),
        compiler_params=pltpu.CompilerParams(vmem_limit_bytes=int(mib * 2**20)),
        cost_estimate=pl.CostEstimate(flops=0, bytes_accessed=0, transcendentals=0),
    )(*ins)


def shape(*dims, dtype=BF16):
    return jax.ShapeDtypeStruct(dims, dtype)


def lanes_of(index, width=LANES):
    return pl.ds(pl.multiple_of(index * width, LANES), width)


def rows_of(index, count):
    return pl.ds(pl.multiple_of(index * count, count), count)


def halves(block):
    half = block.shape[0] // 2
    return jnp.concatenate([block[:half], block[half:]], axis=1)


def keys_body(r, width, latent, rope_t, up_keys, up_values, *refs):
    keys, refs = refs[:H_DEV], refs[H_DEV:]
    latent_v, rope_v, keys_v, values_v, sems = refs
    head_here = lax.axis_index("ctx") // r
    half = width // 2
    moves = [(latent, latent_v), (up_keys, keys_v), (up_values, values_v), (rope_t, rope_v)]
    copies = [pltpu.make_async_copy(a, b, sems.at[i]) for i, (a, b) in enumerate(moves)]
    for copy in copies:
        copy.start()
    for copy in copies:
        copy.wait()
    rope = halves(rope_v[...].T)
    for k in range(H_DEV):
        columns = lanes_of(head_here ^ k)
        up = jnp.concatenate([keys_v[:, columns], values_v[:, columns]], axis=1)
        made = dot(latent_v[...], up).astype(BF16)
        keys[k][0:width] = made[:, :LANES]
        keys[k][width : 2 * width] = made[:, LANES:]
        keys[k][2 * width : 2 * width + half] = rope


def queries_body(r, width, q_nope, q_rope, grad, *queries):
    half = width // 2
    for k in range(H_DEV):
        head = (lax.axis_index("ctx") // r) ^ k
        columns = lanes_of(head)
        queries[k][0:width] = q_nope[:, columns]
        queries[k][width : 2 * width] = grad[:, columns]
        both = q_rope[:, lanes_of(head // 2)]
        mine = jnp.where(head % 2 == 0, both[:, :ROPE], both[:, ROPE:])
        queries[k][2 * width : 2 * width + half] = halves(mine)


def attend_body(n, r, width, order, *refs):
    queries, refs = refs[:H_DEV], refs[H_DEV:]
    pieces, refs = refs[:n], refs[n:]
    kept, refs = refs[:r], refs[r:]
    dq_out, refs = refs[:H_DEV], refs[H_DEV:]
    kcat, kcat_t, vals, qcat, grads, scores, dattn, dq_t, acc, acc_rope, dq_all, table = refs
    me = lax.axis_index("ctx")
    groups = width // GROUP
    half = width // 2
    local = H_DEV * groups
    seq_len = n * width
    chunk = max(2 * GROUP, seq_len // 8)
    depth = LANES + ROPE
    per = TILE // GROUP

    for m in range(n):
        piece = pieces[m]
        for g in range(groups):
            place = order[(me ^ m) * groups + g]
            key = piece[g * GROUP : (g + 1) * GROUP, :]
            packed = piece[2 * width : 2 * width + half, :]
            rope = packed[:, g * ROPE : (g + 1) * ROPE]
            wide = jnp.concatenate([rope, jnp.zeros_like(rope)], axis=1)
            at = rows_of(place, GROUP)
            kcat[at, 0:LANES] = key
            kcat[at, LANES : 2 * LANES] = wide
            kcat_t[0:LANES, lanes_of(place)] = key.T
            kcat_t[LANES : 2 * LANES, lanes_of(place)] = wide.T
            first = width + g * GROUP
            vals[at, :] = piece[first : first + GROUP, :]

    places = [order[(me ^ (k * r)) * groups + g] for k in range(H_DEV) for g in range(groups)]
    ranks = [sum((other < mine).astype(jnp.int32) for other in places) for mine in places]
    for k in range(H_DEV):
        piece = queries[k]
        for g in range(groups):
            rank = ranks[k * groups + g]
            table[rank] = places[k * groups + g]
            at = rows_of(rank, GROUP)
            qcat[at, 0:LANES] = piece[g * GROUP : (g + 1) * GROUP, :]
            rope = piece[2 * width : 2 * width + half, g * ROPE : (g + 1) * ROPE]
            qcat[at, LANES : 2 * LANES] = jnp.concatenate([rope, jnp.zeros_like(rope)], axis=1)
            grads[at, :] = piece[width + g * GROUP : width + (g + 1) * GROUP, :]

    acc[...] = jnp.zeros_like(acc)
    acc_rope[...] = jnp.zeros_like(acc_rope)

    def tile_over(count, t):
        q_rows = rows_of(t, TILE)
        query, grad = qcat[q_rows, :], grads[q_rows, :]
        query_t, grad_t = query.T, grad.T
        lane = lax.broadcasted_iota(jnp.int32, (1, GROUP), 1)
        q_pos = jnp.concatenate([table[per * t + i] * GROUP + lane for i in range(per)], axis=1)
        spans = [slice(c * chunk, (c + 1) * chunk) for c in range(count)]

        def partial(x, how):
            return how(x.reshape(-1, 8, TILE), axis=0)

        top = jnp.full((8, TILE), NEG_LARGE, F32)
        for at in spans:
            raw = dot(kcat[at, :], query_t)
            k_pos = at.start + lax.broadcasted_iota(jnp.int32, (chunk, TILE), 0)
            raw = jnp.where(k_pos <= q_pos, raw, NEG_LARGE)
            scores[at, :] = raw
            top = jnp.maximum(top, partial(raw, jnp.max))
        top = jnp.max(top, axis=0, keepdims=True)
        total = jnp.zeros((8, TILE), F32)
        weighted = jnp.zeros((8, TILE), F32)
        ahead = dot(vals[spans[0], :], grad_t)
        for c, at in enumerate(spans):
            dat = ahead
            if c + 1 < count:
                ahead = dot(vals[spans[c + 1], :], grad_t)
            expd = jnp.exp2((scores[at, :] - top) * SCALE2)
            scores[at, :] = expd
            dattn[at, :] = dat
            total += partial(expd, jnp.sum)
            weighted += partial(expd * dat, jnp.sum)
        inverse = 1.0 / jnp.sum(total, axis=0, keepdims=True)
        delta = jnp.sum(weighted, axis=0, keepdims=True) * inverse

        def weigh(at):
            attn = scores[at, :] * inverse
            return attn.astype(BF16), (attn * (dattn[at, :] - delta)).astype(BF16)

        ahead = weigh(spans[0])
        for c, at in enumerate(spans):
            attn, dscore = ahead
            if c + 1 < count:
                ahead = weigh(spans[c + 1])
            acc[1, at, :] += dot(attn, grad)
            dk = dot(dscore, query)
            acc[0, at, :] += dk[:, 0:LANES]
            acc_rope[at, 0:ROPE] += dk[:, LANES : LANES + ROPE]
            if at.start == 0:
                dq_t[0:depth, :] = dot(kcat_t[0:depth, at], dscore)
            else:
                dq_t[0:depth, :] += dot(kcat_t[0:depth, at], dscore)
        dq_all[q_rows, 0:depth] = (dq_t[0:depth, :] * SCALE).T.astype(BF16)

    def tile(t, carry):
        need = table[per * t + per - 1] // (chunk // GROUP) + 1
        for count in range(1, seq_len // chunk + 1):
            pl.when(need == count)(functools.partial(tile_over, count, t))
        return carry

    lax.fori_loop(0, local // per, tile, 0)

    for k in range(H_DEV):
        out = dq_out[k]
        ropes = []
        for g in range(groups):
            at = rows_of(ranks[k * groups + g], GROUP)
            out[g * GROUP : (g + 1) * GROUP, :] = dq_all[at, 0:LANES]
            ropes.append(dq_all[at, LANES:depth])
        out[width : width + half, :] = jnp.concatenate(ropes, axis=1)

    unit = 2 * width + half
    for j in range(r):
        out = kept[j]
        for k in range(H_DEV):
            ropes = []
            for g in range(groups):
                at = rows_of(order[(me ^ (k * r + j)) * groups + g], GROUP)
                first = k * unit + g * GROUP
                out[first : first + GROUP, :] = (acc[0, at, :] * SCALE).astype(out.dtype)
                out[first + width : first + width + GROUP, :] = acc[1, at, :].astype(out.dtype)
                ropes.append(acc_rope[at, :][:, :ROPE])
            out[k * unit + 2 * width : (k + 1) * unit, :] = (
                jnp.concatenate(ropes, axis=1) * SCALE
            ).astype(out.dtype)


def combine_body(unit, keep, *refs):
    got, outs = refs[:-H_DEV], refs[-H_DEV:]
    for k, out in enumerate(outs):
        rows = slice(k * unit, (k + 1) * unit)
        out[...] = (keep[rows, :] + sum(x[rows, :].astype(F32) for x in got)).astype(BF16)


def weights_body(r, width, rows, *refs):
    latents, refs = refs[:H_DEV], refs[H_DEV:]
    grads, refs = refs[:H_DEV], refs[H_DEV:]
    outs, total = refs[:r], refs[r]
    me = lax.axis_index("ctx")
    value = jnp.zeros(total.shape, F32)
    for k in range(H_DEV):
        pair = jnp.concatenate([grads[k][0:width, :], grads[k][width : 2 * width, :]], axis=1)
        value += dot(latents[k][...], pair, TN)
    total[...] = value
    for j in range(r):
        for k in range(H_DEV):
            part = total[rows_of(me ^ (k * r + j), rows), :].astype(outs[j].dtype)
            first = 2 * k * rows
            outs[j][first : first + rows, :] = part[:, :LANES]
            outs[j][first + rows : first + 2 * rows, :] = part[:, LANES:]


def mix_body(unit, keep, *refs):
    dqs, refs = refs[:H_DEV], refs[H_DEV:]
    got, outs = refs[:-H_DEV], refs[-H_DEV:]
    for k, out in enumerate(outs):
        size = dqs[k].shape[0]
        rows = slice(k * unit, (k + 1) * unit)
        out[0:size, :] = dqs[k][...]
        value = keep[rows, :] + sum(x[rows, :].astype(F32) for x in got)
        out[size : size + unit, :] = value.astype(BF16)


def latent_body(r, width, z_size, *refs):
    own, refs = refs[:H_DEV], refs[H_DEV:]
    up_keys, up_values, kept, *refs = refs
    outs, (total, total_rope) = refs[: z_size - 1], refs[z_size - 1 :]
    me, z = lax.axis_index("ctx"), lax.axis_index("head")
    rope = jnp.zeros((width // 2, LANES), F32)
    value = jnp.zeros(total.shape, F32)
    for k in range(H_DEV):
        head = (me // r) ^ k
        pair = jnp.concatenate([own[k][0:width, :], own[k][width : 2 * width, :]], axis=1)
        up = jnp.concatenate([up_keys[:, lanes_of(head)], up_values[:, lanes_of(head)]], axis=1)
        value += dot(pair, up, NT)
        rope += own[k][2 * width : 2 * width + width // 2, :].astype(F32)
    total[...] = value
    total_rope[...] = rope
    tokens = width // z_size
    blocks = total.shape[1] // LANES
    for k in range(z_size):
        out = kept if k == 0 else outs[k - 1]
        part = total[rows_of(z ^ k, tokens), :].astype(out.dtype)
        for i in range(blocks):
            out[i * tokens : (i + 1) * tokens, :] = part[:, i * LANES : (i + 1) * LANES]
        out[blocks * tokens :, :] = total_rope[rows_of(z ^ k, tokens // 2), :].astype(out.dtype)


def sum_body(kept, *refs):
    *got, out = refs
    out[...] = (kept[...] + sum(x[...].astype(F32) for x in got)).astype(BF16)


def finish_body(z_size, width, *refs):
    parts, (grad_latent, grad_rope_t, rope) = refs[:z_size], refs[z_size:]
    z = lax.axis_index("head")
    tokens = width // z_size
    blocks = grad_latent.shape[1] // LANES
    for k in range(z_size):
        part = parts[k][...].astype(F32)
        for i in range(blocks):
            grad_latent[rows_of(z ^ k, tokens), i * LANES : (i + 1) * LANES] = part[
                i * tokens : (i + 1) * tokens, :
            ]
        rope[rows_of(z ^ k, tokens // 2), :] = part[blocks * tokens :, :]
    both = rope[...].T
    grad_rope_t[:, : width // 2] = both[:ROPE, :]
    grad_rope_t[:, width // 2 :] = both[ROPE:, :]


def unpack_body(r, width, rows, *refs):
    own, refs = refs[:H_DEV], refs[H_DEV:]
    grad_q_nope, grad_q_rope, grad_up_keys, grad_up_values = refs
    me = lax.axis_index("ctx")
    first = width + width // 2
    ropes = []
    for k in range(H_DEV):
        head = (me // r) ^ k
        grad_q_nope[:, lanes_of(head)] = own[k][0:width, :]
        packed = own[k][width:first, :]
        ropes.append(jnp.concatenate([packed[:, :ROPE], packed[:, ROPE:]], axis=0))
        grad_up_keys[:, lanes_of(head)] = own[k][first : first + rows, :].astype(F32)
        grad_up_values[:, lanes_of(head)] = own[k][first + rows : first + 2 * rows, :].astype(F32)
    for k in range(0, H_DEV, 2):
        head = (me // r) ^ k
        a, b = ropes[k], ropes[k + 1]
        even = head % 2 == 0
        grad_q_rope[:, lanes_of(head // 2)] = jnp.concatenate(
            [jnp.where(even, a, b), jnp.where(even, b, a)], axis=1
        )


def attend(n, r, width, group_order, queries, everyone):
    seq_len = n * width
    half = width // 2
    groups = width // GROUP
    unit = 2 * width + half
    rows = H_DEV * width
    return call(
        functools.partial(attend_body, n, r, width),
        [
            shape(H_DEV * unit, LANES, dtype=F32),
            *[shape(H_DEV * unit, LANES)] * (r - 1),
            *[shape(width + half, LANES)] * H_DEV,
        ],
        [group_order, *queries, *everyone],
        scratch=[
            pltpu.VMEM((seq_len, 2 * LANES), BF16),
            pltpu.VMEM((2 * LANES, seq_len), BF16),
            pltpu.VMEM((seq_len, LANES), BF16),
            pltpu.VMEM((rows, 2 * LANES), BF16),
            pltpu.VMEM((rows, LANES), BF16),
            pltpu.VMEM((seq_len, TILE), F32),
            pltpu.VMEM((seq_len, TILE), F32),
            pltpu.VMEM((2 * LANES, TILE), F32),
            pltpu.VMEM((2, seq_len, LANES), F32),
            pltpu.VMEM((seq_len, LANES), F32),
            pltpu.VMEM((rows, 2 * LANES), BF16),
            pltpu.SMEM((H_DEV * groups,), jnp.int32),
        ],
        mib=40,
    )


def per_device(q_nope, q_rope, latent, rope_keys, out_grad, up_keys, up_values, group_order):
    width = q_nope.shape[0]
    depth = latent.shape[1]
    n = lax.axis_size("ctx")
    z_size = lax.axis_size("head")
    r = n // H_DEV
    half = width // 2
    unit = 2 * width + half
    rows = depth // n

    def over_ctx(x, mask):
        return lax.ppermute(x, "ctx", [(i, i ^ mask) for i in range(n)])

    def over_head(x, mask):
        return lax.ppermute(x, "head", [(i, i ^ mask) for i in range(z_size)])

    def across(pieces):
        return [pieces[0]] + [over_ctx(pieces[k], k * r) for k in range(1, H_DEV)]

    def shared(pieces):
        return [over_ctx(p, j) if j else p for p in pieces for j in range(r)]

    def combine(size, parts, mib=16):
        got = [over_ctx(x, j + 1) for j, x in enumerate(parts[1:])]
        return call(
            functools.partial(combine_body, size),
            [shape(size, LANES)] * H_DEV,
            [parts[0], *got],
            mib=mib,
        )

    keys = call(
        functools.partial(keys_body, r, width),
        [shape(unit, LANES)] * H_DEV,
        [latent, rope_keys.T, up_keys, up_values],
        scratch=[
            pltpu.VMEM(latent.shape, BF16),
            pltpu.VMEM((ROPE, width), BF16),
            pltpu.VMEM(up_keys.shape, BF16),
            pltpu.VMEM(up_values.shape, BF16),
            pltpu.SemaphoreType.DMA((4,)),
        ],
        mib=53.1,
        hbm=True,
    )
    queries = call(
        functools.partial(queries_body, r, width),
        [shape(unit, LANES)] * H_DEV,
        [q_nope, q_rope, out_grad],
    )
    arrived = across(keys)
    everyone = shared(arrived)
    queries = across(queries)
    latents = across([latent] * H_DEV)
    outs = attend(n, r, width, group_order, queries, everyone)
    dqs = outs[r:]
    outs, latents = lax.optimization_barrier((outs[:r], latents))
    dkv = combine(unit, outs[:r], mib=24)
    own = across(dkv)

    unit_w = 2 * rows
    parts = call(
        functools.partial(weights_body, r, width, rows),
        [shape(H_DEV * unit_w, LANES, dtype=F32)] + [shape(H_DEV * unit_w, LANES)] * (r - 1),
        [*latents, *dkv],
        scratch=[pltpu.VMEM((depth, 2 * LANES), F32)],
        mib=24,
    )
    got = [over_ctx(x, j + 1) for j, x in enumerate(parts[1:])]
    ready = call(
        functools.partial(mix_body, unit_w),
        [shape(width + half + unit_w, LANES)] * H_DEV,
        [parts[0], *dqs, *got],
    )
    mixed = across(ready)
    up_keys = lax.optimization_barrier((up_keys, ready))[0]

    tokens = width // z_size
    z_rows = depth // LANES * tokens + tokens // 2
    kept, *for_planes = call(
        functools.partial(latent_body, r, width, z_size),
        [shape(z_rows, LANES, dtype=F32)] + [shape(z_rows, LANES)] * (z_size - 1),
        [*own, up_keys, up_values],
        scratch=[pltpu.VMEM((width, depth), F32), pltpu.VMEM((half, LANES), F32)],
    )
    received = [over_head(x, k + 1) for k, x in enumerate(for_planes)]
    (part,) = call(sum_body, [shape(z_rows, LANES)], [kept, *received])
    parts = [part] + [over_head(part, k) for k in range(1, z_size)]
    grad_latent, grad_rope_t = call(
        functools.partial(finish_body, z_size, width),
        [shape(width, depth, dtype=F32), shape(ROPE, width, dtype=F32)],
        parts,
        scratch=[pltpu.VMEM((half, LANES), F32)],
    )

    grad_q_nope, grad_q_rope, grad_up_keys, grad_up_values = call(
        functools.partial(unpack_body, r, width, rows),
        [
            shape(width, H_DEV * HEAD_DIM),
            shape(width, H_DEV * ROPE),
            shape(rows, H_DEV * HEAD_DIM, dtype=F32),
            shape(rows, H_DEV * HEAD_DIM, dtype=F32),
        ],
        mixed,
    )
    return (grad_q_nope, grad_q_rope, grad_latent, grad_rope_t.T, grad_up_keys, grad_up_values)


def solution(mesh):
    in_specs = (
        P("ctx", "head"),
        P("ctx", "head"),
        P("ctx", None),
        P("ctx", None),
        P("ctx", "head"),
        P(None, "head"),
        P(None, "head"),
        P(),
    )
    out_specs = (
        P("ctx", "head"),
        P("ctx", "head"),
        P("ctx", None),
        P("ctx", None),
        P("ctx", "head"),
        P("ctx", "head"),
    )
    return jax.shard_map(
        per_device, mesh=mesh, in_specs=in_specs, out_specs=out_specs, check_vma=False
    )
```

```python
import functools
import math

import jax
import jax.numpy as jnp
from jax import lax
from jax.experimental import pallas as pl
from jax.experimental.pallas import tpu as pltpu
from jax.sharding import PartitionSpec as P

ROPE = 64
HEAD_DIM = 128
H_DEV = 4
GROUP = 128
LANES = 128
TILE = 4 * GROUP
SCALE = (HEAD_DIM + ROPE) ** (-0.5)
SCALE2 = SCALE * math.log2(math.e)
NEG_LARGE = -1e30

F32 = jnp.float32
BF16 = jnp.bfloat16
NT = (((1,), (1,)), ((), ()))
TN = (((0,), (0,)), ((), ()))
NN = (((1,), (0,)), ((), ()))
VMEM = pl.BlockSpec(memory_space=pltpu.VMEM)
SMEM = pl.BlockSpec(memory_space=pltpu.SMEM)
HBM = pl.BlockSpec(memory_space=pltpu.HBM)


def dot(a, b, dims=NN):
    return lax.dot_general(a, b, dims, preferred_element_type=F32)


def call(body, outs, ins, scratch=(), mib=16, hbm=()):
    return pl.pallas_call(
        body,
        out_shape=list(outs),
        in_specs=[
            SMEM if x.dtype == jnp.int32 else HBM if i in hbm else VMEM for i, x in enumerate(ins)
        ],
        out_specs=[VMEM] * len(outs),
        scratch_shapes=list(scratch),
        compiler_params=pltpu.CompilerParams(vmem_limit_bytes=int(mib * 2**20)),
        cost_estimate=pl.CostEstimate(flops=0, bytes_accessed=0, transcendentals=0),
    )(*ins)


def shape(*dims, dtype=BF16):
    return jax.ShapeDtypeStruct(dims, dtype)


def lanes_of(index, width=LANES):
    return pl.ds(pl.multiple_of(index * width, LANES), width)


def rows_of(index, count):
    return pl.ds(pl.multiple_of(index * count, count), count)


def halves(block):
    half = block.shape[0] // 2
    return jnp.concatenate([block[:half], block[half:]], axis=1)


def keys_body(r, width, latent, rope_t, up_keys, up_values, *refs):
    keys, refs = refs[:H_DEV], refs[H_DEV:]
    latent_v, keys_v, values_v, sems = refs
    head_here = lax.axis_index("ctx") // r
    half = width // 2
    moves = [(latent, latent_v), (up_keys, keys_v), (up_values, values_v)]
    copies = [pltpu.make_async_copy(a, b, sems.at[i]) for i, (a, b) in enumerate(moves)]
    for copy in copies:
        copy.start()
    rope = halves(rope_t[...].T)
    for k in range(H_DEV):
        keys[k][2 * width : 2 * width + half] = rope
    copies[0].wait()
    for copy, up, first in ((copies[1], keys_v, 0), (copies[2], values_v, width)):
        copy.wait()
        for k in range(0, H_DEV, 2):
            pair = [up[:, lanes_of(head_here ^ i)] for i in (k, k + 1)]
            made = dot(latent_v[...], jnp.concatenate(pair, axis=1)).astype(BF16)
            keys[k][first : first + width] = made[:, :LANES]
            keys[k + 1][first : first + width] = made[:, LANES:]


def queries_body(r, width, q_nope, q_rope, grad, *queries):
    half = width // 2
    for k in range(H_DEV):
        head = (lax.axis_index("ctx") // r) ^ k
        columns = lanes_of(head)
        queries[k][0:width] = q_nope[:, columns]
        queries[k][width : 2 * width] = grad[:, columns]
        both = q_rope[:, lanes_of(head // 2)]
        mine = jnp.where(head % 2 == 0, both[:, :ROPE], both[:, ROPE:])
        queries[k][2 * width : 2 * width + half] = halves(mine)


def attend_body(n, r, width, order, *refs):
    queries, refs = refs[:H_DEV], refs[H_DEV:]
    pieces, refs = refs[:n], refs[n:]
    kept, refs = refs[:r], refs[r:]
    dq_out, refs = refs[:H_DEV], refs[H_DEV:]
    kcat, kcat_t, vals, qcat, grads, scores, dattn, dq_t, acc, acc_rope, dq_all, table = refs
    me = lax.axis_index("ctx")
    groups = width // GROUP
    half = width // 2
    local = H_DEV * groups
    seq_len = n * width
    chunk = max(2 * GROUP, seq_len // 8)
    depth = LANES + ROPE
    per = TILE // GROUP

    for m in range(n):
        piece = pieces[m]
        for g in range(groups):
            place = order[(me ^ m) * groups + g]
            key = piece[g * GROUP : (g + 1) * GROUP, :]
            packed = piece[2 * width : 2 * width + half, :]
            rope = packed[:, g * ROPE : (g + 1) * ROPE]
            wide = jnp.concatenate([rope, jnp.zeros_like(rope)], axis=1)
            at = rows_of(place, GROUP)
            kcat[at, 0:LANES] = key
            kcat[at, LANES : 2 * LANES] = wide
            kcat_t[0:LANES, lanes_of(place)] = key.T
            kcat_t[LANES : 2 * LANES, lanes_of(place)] = wide.T
            first = width + g * GROUP
            vals[at, :] = piece[first : first + GROUP, :]

    places = [order[(me ^ (k * r)) * groups + g] for k in range(H_DEV) for g in range(groups)]
    ranks = [sum((other < mine).astype(jnp.int32) for other in places) for mine in places]
    for k in range(H_DEV):
        piece = queries[k]
        for g in range(groups):
            rank = ranks[k * groups + g]
            table[rank] = places[k * groups + g]
            at = rows_of(rank, GROUP)
            qcat[at, 0:LANES] = piece[g * GROUP : (g + 1) * GROUP, :]
            rope = piece[2 * width : 2 * width + half, g * ROPE : (g + 1) * ROPE]
            qcat[at, LANES : 2 * LANES] = jnp.concatenate([rope, jnp.zeros_like(rope)], axis=1)
            grads[at, :] = piece[width + g * GROUP : width + (g + 1) * GROUP, :]

    acc[...] = jnp.zeros_like(acc)
    acc_rope[...] = jnp.zeros_like(acc_rope)

    def tile_over(count, t):
        q_rows = rows_of(t, TILE)
        query, grad = qcat[q_rows, :], grads[q_rows, :]
        query_t, grad_t = query.T, grad.T
        lane = lax.broadcasted_iota(jnp.int32, (1, GROUP), 1)
        q_pos = jnp.concatenate([table[per * t + i] * GROUP + lane for i in range(per)], axis=1)
        spans = [slice(c * chunk, (c + 1) * chunk) for c in range(count)]

        def partial(x, how):
            return how(x.reshape(-1, 8, TILE), axis=0)

        top = jnp.full((8, TILE), NEG_LARGE, F32)
        for at in spans:
            raw = dot(kcat[at, :], query_t)
            k_pos = at.start + lax.broadcasted_iota(jnp.int32, (chunk, TILE), 0)
            raw = jnp.where(k_pos <= q_pos, raw, NEG_LARGE)
            scores[at, :] = raw
            top = jnp.maximum(top, partial(raw, jnp.max))
        top = jnp.max(top, axis=0, keepdims=True)
        total = jnp.zeros((8, TILE), F32)
        weighted = jnp.zeros((8, TILE), F32)
        ahead = dot(vals[spans[0], :], grad_t)
        for c, at in enumerate(spans):
            dat = ahead
            if c + 1 < count:
                ahead = dot(vals[spans[c + 1], :], grad_t)
            expd = jnp.exp2((scores[at, :] - top) * SCALE2)
            scores[at, :] = expd
            dattn[at, :] = dat
            total += partial(expd, jnp.sum)
            weighted += partial(expd * dat, jnp.sum)
        inverse = 1.0 / jnp.sum(total, axis=0, keepdims=True)
        delta = jnp.sum(weighted, axis=0, keepdims=True) * inverse

        def weigh(at):
            attn = scores[at, :] * inverse
            return attn.astype(BF16), (attn * (dattn[at, :] - delta)).astype(BF16)

        ahead = weigh(spans[0])
        for c, at in enumerate(spans):
            attn, dscore = ahead
            if c + 1 < count:
                ahead = weigh(spans[c + 1])
            acc[1, at, :] += dot(attn, grad)
            dk = dot(dscore, query)
            acc[0, at, :] += dk[:, 0:LANES]
            acc_rope[at, 0:ROPE] += dk[:, LANES : LANES + ROPE]
            if at.start == 0:
                dq_t[0:depth, :] = dot(kcat_t[0:depth, at], dscore)
            else:
                dq_t[0:depth, :] += dot(kcat_t[0:depth, at], dscore)
        dq_all[q_rows, 0:depth] = (dq_t[0:depth, :] * SCALE).T.astype(BF16)

    def tile(t, carry):
        need = table[per * t + per - 1] // (chunk // GROUP) + 1
        for count in range(1, seq_len // chunk + 1):
            pl.when(need == count)(functools.partial(tile_over, count, t))
        return carry

    lax.fori_loop(0, local // per, tile, 0)

    for k in range(H_DEV):
        out = dq_out[k]
        ropes = []
        for g in range(groups):
            at = rows_of(ranks[k * groups + g], GROUP)
            out[g * GROUP : (g + 1) * GROUP, :] = dq_all[at, 0:LANES]
            ropes.append(dq_all[at, LANES:depth])
        out[width : width + half, :] = jnp.concatenate(ropes, axis=1)

    unit = 2 * width + half
    for j in range(r):
        out = kept[j]
        for k in range(H_DEV):
            ropes = []
            for g in range(groups):
                at = rows_of(order[(me ^ (k * r + j)) * groups + g], GROUP)
                first = k * unit + g * GROUP
                out[first : first + GROUP, :] = (acc[0, at, :] * SCALE).astype(out.dtype)
                out[first + width : first + width + GROUP, :] = acc[1, at, :].astype(out.dtype)
                ropes.append(acc_rope[at, :][:, :ROPE])
            out[k * unit + 2 * width : (k + 1) * unit, :] = (
                jnp.concatenate(ropes, axis=1) * SCALE
            ).astype(out.dtype)


def combine_body(unit, keep, *refs):
    got, outs = refs[:-H_DEV], refs[-H_DEV:]
    for k, out in enumerate(outs):
        rows = slice(k * unit, (k + 1) * unit)
        out[...] = (keep[rows, :] + sum(x[rows, :].astype(F32) for x in got)).astype(BF16)


def weights_body(r, width, rows, *refs):
    latents, refs = refs[:H_DEV], refs[H_DEV:]
    grads, refs = refs[:H_DEV], refs[H_DEV:]
    outs, total = refs[:r], refs[r]
    me = lax.axis_index("ctx")
    value = jnp.zeros(total.shape, F32)
    for k in range(H_DEV):
        pair = jnp.concatenate([grads[k][0:width, :], grads[k][width : 2 * width, :]], axis=1)
        value += dot(latents[k][...], pair, TN)
    total[...] = value
    for j in range(r):
        for k in range(H_DEV):
            part = total[rows_of(me ^ (k * r + j), rows), :].astype(outs[j].dtype)
            first = 2 * k * rows
            outs[j][first : first + rows, :] = part[:, :LANES]
            outs[j][first + rows : first + 2 * rows, :] = part[:, LANES:]


def mix_body(unit, keep, *refs):
    dqs, refs = refs[:H_DEV], refs[H_DEV:]
    got, outs = refs[:-H_DEV], refs[-H_DEV:]
    for k, out in enumerate(outs):
        size = dqs[k].shape[0]
        rows = slice(k * unit, (k + 1) * unit)
        out[0:size, :] = dqs[k][...]
        value = keep[rows, :] + sum(x[rows, :].astype(F32) for x in got)
        out[size : size + unit, :] = value.astype(BF16)


def latent_body(r, width, z_size, *refs):
    own, refs = refs[:H_DEV], refs[H_DEV:]
    up_keys, up_values, kept, *refs = refs
    outs, (total, total_rope) = refs[: z_size - 1], refs[z_size - 1 :]
    me, z = lax.axis_index("ctx"), lax.axis_index("head")
    rope = jnp.zeros((width // 2, LANES), F32)
    value = jnp.zeros(total.shape, F32)
    for k in range(H_DEV):
        head = (me // r) ^ k
        pair = jnp.concatenate([own[k][0:width, :], own[k][width : 2 * width, :]], axis=1)
        up = jnp.concatenate([up_keys[:, lanes_of(head)], up_values[:, lanes_of(head)]], axis=1)
        value += dot(pair, up, NT)
        rope += own[k][2 * width : 2 * width + width // 2, :].astype(F32)
    total[...] = value
    total_rope[...] = rope
    tokens = width // z_size
    blocks = total.shape[1] // LANES
    for k in range(z_size):
        out = kept if k == 0 else outs[k - 1]
        part = total[rows_of(z ^ k, tokens), :].astype(out.dtype)
        for i in range(blocks):
            out[i * tokens : (i + 1) * tokens, :] = part[:, i * LANES : (i + 1) * LANES]
        out[blocks * tokens :, :] = total_rope[rows_of(z ^ k, tokens // 2), :].astype(out.dtype)


def sum_body(kept, *refs):
    *got, out = refs
    out[...] = (kept[...] + sum(x[...].astype(F32) for x in got)).astype(BF16)


def finish_body(z_size, width, *refs):
    parts, (grad_latent, grad_rope_t, rope) = refs[:z_size], refs[z_size:]
    z = lax.axis_index("head")
    tokens = width // z_size
    blocks = grad_latent.shape[1] // LANES
    for k in range(z_size):
        part = parts[k][...].astype(F32)
        for i in range(blocks):
            grad_latent[rows_of(z ^ k, tokens), i * LANES : (i + 1) * LANES] = part[
                i * tokens : (i + 1) * tokens, :
            ]
        rope[rows_of(z ^ k, tokens // 2), :] = part[blocks * tokens :, :]
    both = rope[...].T
    grad_rope_t[:, : width // 2] = both[:ROPE, :]
    grad_rope_t[:, width // 2 :] = both[ROPE:, :]


def unpack_body(r, width, rows, *refs):
    own, refs = refs[:H_DEV], refs[H_DEV:]
    grad_q_nope, grad_q_rope, grad_up_keys, grad_up_values = refs
    me = lax.axis_index("ctx")
    first = width + width // 2
    ropes = []
    for k in range(H_DEV):
        head = (me // r) ^ k
        grad_q_nope[:, lanes_of(head)] = own[k][0:width, :]
        packed = own[k][width:first, :]
        ropes.append(jnp.concatenate([packed[:, :ROPE], packed[:, ROPE:]], axis=0))
        grad_up_keys[:, lanes_of(head)] = own[k][first : first + rows, :].astype(F32)
        grad_up_values[:, lanes_of(head)] = own[k][first + rows : first + 2 * rows, :].astype(F32)
    for k in range(0, H_DEV, 2):
        head = (me // r) ^ k
        a, b = ropes[k], ropes[k + 1]
        even = head % 2 == 0
        grad_q_rope[:, lanes_of(head // 2)] = jnp.concatenate(
            [jnp.where(even, a, b), jnp.where(even, b, a)], axis=1
        )


def attend(n, r, width, group_order, queries, everyone):
    seq_len = n * width
    half = width // 2
    groups = width // GROUP
    unit = 2 * width + half
    rows = H_DEV * width
    return call(
        functools.partial(attend_body, n, r, width),
        [
            shape(H_DEV * unit, LANES, dtype=F32),
            *[shape(H_DEV * unit, LANES)] * (r - 1),
            *[shape(width + half, LANES)] * H_DEV,
        ],
        [group_order, *queries, *everyone],
        scratch=[
            pltpu.VMEM((seq_len, 2 * LANES), BF16),
            pltpu.VMEM((2 * LANES, seq_len), BF16),
            pltpu.VMEM((seq_len, LANES), BF16),
            pltpu.VMEM((rows, 2 * LANES), BF16),
            pltpu.VMEM((rows, LANES), BF16),
            pltpu.VMEM((seq_len, TILE), F32),
            pltpu.VMEM((seq_len, TILE), F32),
            pltpu.VMEM((2 * LANES, TILE), F32),
            pltpu.VMEM((2, seq_len, LANES), F32),
            pltpu.VMEM((seq_len, LANES), F32),
            pltpu.VMEM((rows, 2 * LANES), BF16),
            pltpu.SMEM((H_DEV * groups,), jnp.int32),
        ],
        mib=40,
    )


def per_device(q_nope, q_rope, latent, rope_keys, out_grad, up_keys, up_values, group_order):
    width = q_nope.shape[0]
    depth = latent.shape[1]
    n = lax.axis_size("ctx")
    z_size = lax.axis_size("head")
    r = n // H_DEV
    half = width // 2
    unit = 2 * width + half
    rows = depth // n

    def over_ctx(x, mask):
        return lax.ppermute(x, "ctx", [(i, i ^ mask) for i in range(n)])

    def over_head(x, mask):
        return lax.ppermute(x, "head", [(i, i ^ mask) for i in range(z_size)])

    def across(pieces):
        return [pieces[0]] + [over_ctx(pieces[k], k * r) for k in range(1, H_DEV)]

    def shared(pieces):
        return [over_ctx(p, j) if j else p for p in pieces for j in range(r)]

    def combine(size, parts, mib=16):
        got = [over_ctx(x, j + 1) for j, x in enumerate(parts[1:])]
        return call(
            functools.partial(combine_body, size),
            [shape(size, LANES)] * H_DEV,
            [parts[0], *got],
            mib=mib,
        )

    keys = call(
        functools.partial(keys_body, r, width),
        [shape(unit, LANES)] * H_DEV,
        [latent, rope_keys.T, up_keys, up_values],
        scratch=[
            pltpu.VMEM(latent.shape, BF16),
            pltpu.VMEM(up_keys.shape, BF16),
            pltpu.VMEM(up_values.shape, BF16),
            pltpu.SemaphoreType.DMA((3,)),
        ],
        mib=53.1,
        hbm=(0, 2, 3),
    )
    queries = call(
        functools.partial(queries_body, r, width),
        [shape(unit, LANES)] * H_DEV,
        [q_nope, q_rope, out_grad],
    )
    arrived = across(keys)
    everyone = shared(arrived)
    queries = across(queries)
    latents = across([latent] * H_DEV)
    outs = attend(n, r, width, group_order, queries, everyone)
    dqs = outs[r:]
    outs, latents = lax.optimization_barrier((outs[:r], latents))
    dkv = combine(unit, outs[:r], mib=24)
    own = across(dkv)

    unit_w = 2 * rows
    parts = call(
        functools.partial(weights_body, r, width, rows),
        [shape(H_DEV * unit_w, LANES, dtype=F32)] + [shape(H_DEV * unit_w, LANES)] * (r - 1),
        [*latents, *dkv],
        scratch=[pltpu.VMEM((depth, 2 * LANES), F32)],
        mib=24,
    )
    got = [over_ctx(x, j + 1) for j, x in enumerate(parts[1:])]
    ready = call(
        functools.partial(mix_body, unit_w),
        [shape(width + half + unit_w, LANES)] * H_DEV,
        [parts[0], *dqs, *got],
    )
    mixed = across(ready)
    up_keys = lax.optimization_barrier((up_keys, ready))[0]

    tokens = width // z_size
    z_rows = depth // LANES * tokens + tokens // 2
    kept, *for_planes = call(
        functools.partial(latent_body, r, width, z_size),
        [shape(z_rows, LANES, dtype=F32)] + [shape(z_rows, LANES)] * (z_size - 1),
        [*own, up_keys, up_values],
        scratch=[pltpu.VMEM((width, depth), F32), pltpu.VMEM((half, LANES), F32)],
    )
    received = [over_head(x, k + 1) for k, x in enumerate(for_planes)]
    (part,) = call(sum_body, [shape(z_rows, LANES)], [kept, *received])
    parts = [part] + [over_head(part, k) for k in range(1, z_size)]
    grad_latent, grad_rope_t = call(
        functools.partial(finish_body, z_size, width),
        [shape(width, depth, dtype=F32), shape(ROPE, width, dtype=F32)],
        parts,
        scratch=[pltpu.VMEM((half, LANES), F32)],
    )

    grad_q_nope, grad_q_rope, grad_up_keys, grad_up_values = call(
        functools.partial(unpack_body, r, width, rows),
        [
            shape(width, H_DEV * HEAD_DIM),
            shape(width, H_DEV * ROPE),
            shape(rows, H_DEV * HEAD_DIM, dtype=F32),
            shape(rows, H_DEV * HEAD_DIM, dtype=F32),
        ],
        mixed,
    )
    return (grad_q_nope, grad_q_rope, grad_latent, grad_rope_t.T, grad_up_keys, grad_up_values)


def solution(mesh):
    in_specs = (
        P("ctx", "head"),
        P("ctx", "head"),
        P("ctx", None),
        P("ctx", None),
        P("ctx", "head"),
        P(None, "head"),
        P(None, "head"),
        P(),
    )
    out_specs = (
        P("ctx", "head"),
        P("ctx", "head"),
        P("ctx", None),
        P("ctx", None),
        P("ctx", "head"),
        P("ctx", "head"),
    )
    return jax.shard_map(
        per_device, mesh=mesh, in_specs=in_specs, out_specs=out_specs, check_vma=False
    )
```
